512 devices in a mesh: lon: 32 (over x_lo, y, core), lat: 16 (over z, x_hi).
Axes of the slice: x: 4 (x_hi: 2, x_lo: 2; x = x_hi * 2 + x_lo), y: 8, z: 8, core: 2. Of those that a mesh axis runs over, the one named last changes fastest.
Arguments:
- potential_warmth: float32 [25, 256, 4096], P(None, 'lat', 'lon'), may hold values from -4 to 4
- saltiness_anomaly: float32 [25, 256, 4096], P(None, 'lat', 'lon'), may hold values from -4 to 4
- east_speed_array: float32 [25, 256, 4096], P(None, 'lat', 'lon'), may hold values from -1 to 1
- north_speed_array: float32 [25, 256, 4096], P(None, 'lat', 'lon'), may hold values from -1 to 1
- water_indicator: int32 [25, 256, 4096], P(None, 'lat', 'lon'), may hold values from 0 to 1, as said below
- bottom_layer_index: int32 [256, 4096], P('lat', 'lon'), may hold values from 0 to 25, as said below
Outputs:
- temperature_next: float32 [25, 256, 4096], P(None, 'lat', 'lon')
- salinity_next: float32 [25, 256, 4096], P(None, 'lat', 'lon')
- zonal_next: float32 [25, 256, 4096], P(None, 'lat', 'lon')
- meridional_next: float32 [25, 256, 4096], P(None, 'lat', 'lon')
The draws below stay inside these ranges and needn't reach their ends.
Inputs may be any that keep to these rules, and one draw needn't show every extreme that they name: `bottom_layer_index`: 0 marks a land column; a sea column has this many wet levels. `water_indicator`: 1 exactly at the levels k of a column with k < bottom_layer_index of that column.
All inputs are finite; a program needn't handle non-finite values.
Results may differ from the reference program's by a relative error of at most 0.00016.
Values sent between devices are 32-bit elements; how exact they have to be, the bound alone decides.
A program may use at most 64 MiB of HBM per device.

```python
import jax
import jax.numpy as jnp

DEPTH_LAYERS = 25
SWEEPS = 4
PARALLEL_LINES = 256
MERIDIAN_LINES = 4096


def column_floor(key):
    raw_level = jax.random.randint(key, (PARALLEL_LINES, MERIDIAN_LINES), -(DEPTH_LAYERS // 3), DEPTH_LAYERS + 1)
    return jnp.maximum(raw_level, 0).astype(jnp.int32)


def draw_bottom_layer_index(key, part):
    return column_floor(key)


def draw_water_indicator(key, part):
    floor_level = column_floor(key)
    level_ids = jnp.arange(DEPTH_LAYERS, dtype=jnp.int32)[:, None, None]
    return (level_ids < floor_level[None]).astype(jnp.int32)


def block_scale(key, dims, split, low, largest):
    loudness = 1.0
    for position, parts in split:
        heights = jax.random.uniform(jax.random.fold_in(jax.random.fold_in(key, 6), position), (parts,), jnp.float32, low / len(split), largest / len(split))
        loudness = loudness * jnp.repeat(jnp.exp(heights), dims[position] // parts).reshape((-1,) + (1,) * (len(dims) - 1 - position))
    return loudness


def gaussian(key, extent, deviation, reach, split=(), kind=jnp.bfloat16):
    array = jax.random.normal(key, extent, jnp.float32) * deviation
    if len(split) > 0:
        array = block_scale(key, extent, split, -0.22, 0.18) * array
    return jnp.clip(array, min=-reach, max=reach).astype(kind)


def setup_inputs(seed: int = 0) -> dict:
    key_of = jax.random.split(jax.random.key(seed), 7)
    return {
        "potential_warmth": gaussian(key_of[0], (DEPTH_LAYERS, PARALLEL_LINES, MERIDIAN_LINES), 1.0, 4.0, ((1, 16), (2, 32)), jnp.float32),
        "saltiness_anomaly": gaussian(key_of[1], (DEPTH_LAYERS, PARALLEL_LINES, MERIDIAN_LINES), 1.0, 4.0, ((1, 16), (2, 32)), jnp.float32),
        "east_speed_array": jnp.clip(jax.random.uniform(key_of[2], (DEPTH_LAYERS, PARALLEL_LINES, MERIDIAN_LINES), jnp.float32, -1.0, 1.0) * block_scale(key_of[2], (DEPTH_LAYERS, PARALLEL_LINES, MERIDIAN_LINES), ((1, 16), (2, 32)), -0.4, 0.0), -1.0, 1.0),
        "north_speed_array": jnp.clip(jax.random.uniform(key_of[3], (DEPTH_LAYERS, PARALLEL_LINES, MERIDIAN_LINES), jnp.float32, -1.0, 1.0) * block_scale(key_of[3], (DEPTH_LAYERS, PARALLEL_LINES, MERIDIAN_LINES), ((1, 16), (2, 32)), -0.4, 0.0), -1.0, 1.0),
        "water_indicator": draw_water_indicator(jax.random.fold_in(key_of[6], 71), 0),
        "bottom_layer_index": draw_bottom_layer_index(jax.random.fold_in(key_of[6], 71), 0),
    }


courant = 0.3
mixing = 0.08
vertical_mixing = 0.1
buoyancy = 0.05
rotation = 0.2
drag_rate = 0.3
thermal = 0.25
haline = 0.2
cabbeling = 0.03


def neighbours(field, sign):
    east = jnp.roll(field, -1, axis=-1)
    west = jnp.roll(field, 1, axis=-1)
    south = jnp.concatenate([jnp.zeros_like(field[..., :1, :]), field[..., :-1, :]], axis=-2)
    north = jnp.concatenate([field[..., 1:, :], sign * field[..., -1:, ::-1]], axis=-2)
    return east, west, north, south


def vertical_terms(field, upper_open, lower_open):
    above = jnp.concatenate([field[:1], field[:-1]], axis=0)
    below = jnp.concatenate([field[1:], field[-1:]], axis=0)
    return upper_open * (above - field) + lower_open * (below - field)


def transport(field, east, west, north, south, faces, cross_x, cross_y):
    open_east, open_west, open_north, open_south = faces
    advection = (jnp.maximum(cross_x, 0.0) * open_west * (field - west)
                 + jnp.minimum(cross_x, 0.0) * open_east * (east - field)
                 + jnp.maximum(cross_y, 0.0) * open_south * (field - south)
                 + jnp.minimum(cross_y, 0.0) * open_north * (north - field))
    diffusion = (open_east * (east - field) + open_west * (west - field)
                 + open_north * (north - field) + open_south * (south - field))
    return mixing * diffusion - advection


def reference(potential_warmth, saltiness_anomaly, east_speed_array, north_speed_array, water_indicator, bottom_layer_index):
    wet = water_indicator.astype(jnp.float32)
    level_ids = jnp.arange(DEPTH_LAYERS, dtype=jnp.int32)[:, None, None]
    deep = (level_ids < bottom_layer_index[None]).astype(jnp.float32)
    deep_east, deep_west, deep_north, deep_south = neighbours(deep, 1.0)
    faces = (deep * deep_east, deep * deep_west, deep * deep_north, deep * deep_south)
    zero_level = jnp.zeros_like(wet[:1])
    upper_open = wet * jnp.concatenate([zero_level, wet[:-1]], axis=0)
    lower_open = wet * jnp.concatenate([wet[1:], zero_level], axis=0)
    drag = 1.0 - drag_rate * (level_ids == bottom_layer_index[None] - 1).astype(jnp.float32)
    row_ids = jnp.arange(PARALLEL_LINES, dtype=jnp.float32)[:, None]
    coriolis = rotation * (2.0 * (row_ids + 0.5) / PARALLEL_LINES - 1.0)
    signs = (1.0, 1.0, -1.0, -1.0)
    thermal_energy, saltiness_values, west_east_current, south_north_current = potential_warmth, saltiness_anomaly, east_speed_array, north_speed_array
    for sweep_step in range(SWEEPS):
        fields = (thermal_energy, saltiness_values, west_east_current, south_north_current)
        density = -thermal * thermal_energy + haline * saltiness_values - cabbeling * thermal_energy * thermal_energy
        pressure = buoyancy * jnp.cumsum(density, axis=0)
        p_east, p_west, p_north, p_south = neighbours(pressure, 1.0)
        grad_x = 0.5 * (faces[0] * (p_east - pressure) + faces[1] * (pressure - p_west))
        grad_y = 0.5 * (faces[2] * (p_north - pressure) + faces[3] * (pressure - p_south))
        cross_x = courant * west_east_current
        cross_y = courant * south_north_current
        updated = []
        for member in range(4):
            field = fields[member]
            east, west, north, south = neighbours(field, signs[member])
            change = transport(field, east, west, north, south, faces, cross_x, cross_y)
            change = change + vertical_mixing * vertical_terms(field, upper_open, lower_open)
            updated.append(field + change)
        heat_new = wet * updated[0]
        salt_new = wet * updated[1]
        zonal_new = wet * drag * (updated[2] + coriolis * south_north_current - grad_x)
        meridional_new = wet * drag * (updated[3] - coriolis * west_east_current - grad_y)
        thermal_energy, saltiness_values, west_east_current, south_north_current = heat_new, salt_new, zonal_new, meridional_new
    return (thermal_energy, saltiness_values, west_east_current, south_north_current)
```

```python
import functools

import jax
import jax.numpy as jnp
from jax import lax
from jax.experimental import pallas as pl
from jax.experimental.pallas import tpu as pltpu
from jax.sharding import PartitionSpec as P

SWEEPS = 4

courant = 0.3
mixing = 0.08
vertical_mixing = 0.1
buoyancy = 0.05
rotation = 0.2
drag_rate = 0.3
thermal = 0.25
haline = 0.2
cabbeling = 0.03

K = 25
R = 16
G = 4
LIN = (R + 2 * G) * K + 16
BLOCK = 56
HEAD = 8
CHUNKS = ((0, 112), (112, 96), (208, 104), (312, 96))
MSG = 408
PACKED = 104
CORNER = 32
KB = (0, 8, 16, 17)
N_MASK = 8

LON, LAT = "lon", "lat"


def lane(shape):
    return lax.broadcasted_iota(jnp.int32, shape, 1)


def density(t, s):
    h = 0.5 * buoyancy
    return t * (-thermal * h - (cabbeling * h) * t) + (haline * h) * s


def kernel(
    n_lon, n_lat, t_hbm, s_hbm, u_hbm, v_hbm, b_hbm, out_hbm,
    xin, bin_, m_st, q_st, m4, pm, pq, mk, qk, cor, bm, bq,
    pack, pack_w, pack_e, send_n, send_s, recv_n, recv_s, csend_n, csend_s, crecv_n, crecv_s,
    in_sem, out_sem, lon_ss, lon_rs, n_ss, n_rs, s_ss, s_rs,
):
    i = lax.axis_index(LON)
    j = lax.axis_index(LAT)
    top = j == n_lat - 1
    east = lax.rem(i + 1, n_lon)
    west = lax.rem(i + n_lon - 1, n_lon)
    has_south = j > 0
    north = {LON: jnp.where(top, n_lon - 1 - i, i), LAT: jnp.where(top, j, j + 1)}
    south = {LON: i, LAT: jnp.maximum(j - 1, 0)}
    mesh_id = pl.DeviceIdType.MESH

    barrier = pltpu.get_barrier_semaphore()
    pl.semaphore_signal(barrier, inc=1, device_id={LON: east, LAT: j}, device_id_type=mesh_id)
    pl.semaphore_signal(barrier, inc=1, device_id={LON: west, LAT: j}, device_id_type=mesh_id)
    pl.semaphore_signal(barrier, inc=1, device_id=north, device_id_type=mesh_id)

    @pl.when(has_south)
    def _():
        pl.semaphore_signal(barrier, inc=1, device_id=south, device_id_type=mesh_id)

    loads = [
        pltpu.make_async_copy(ref, xin.at[f], in_sem.at[f])
        for f, ref in enumerate((t_hbm, s_hbm, u_hbm, v_hbm))
    ]
    loads.append(pltpu.make_async_copy(b_hbm, bin_, in_sem.at[4]))
    for c in loads:
        c.start()
    for c in loads:
        c.wait()

    lanes8 = lane((8, 128))
    group8 = lanes8 // 8

    bm[pl.ds(G, R), :] = bin_[...].astype(jnp.float32)
    tiles = [(f, k, h) for f in range(4) for k in range(K) for h in range(2)]
    tiles += [(4, 0, 0), (4, 0, 1)]
    acc = None
    for n, (f, k, h) in enumerate(tiles):
        if f < 4:
            v = xin[f, k, pl.ds(8 * h, 8), :]
            m_st[0, f, pl.ds((G + 8 * h) * K + k, 8, stride=K), :] = v
        else:
            v = bm[pl.ds(G + 8 * h, 8), :]
        g = n % 16
        rolled = pltpu.roll(v, 4 + 8 * g, 1)
        acc = rolled if g == 0 else jnp.where(group8 == g, rolled, acc)
        if g == 15 or n == len(tiles) - 1:
            pack[pl.ds(8 * (n // 16), 8), :] = acc

    sign = jnp.where(top, -1.0, 1.0).astype(jnp.float32)
    lanes32 = lane((32, 128))
    turn32 = jnp.where(top, 127 - lanes32, lanes32)
    turn8 = jnp.where(top, 127 - lanes8, lanes8)
    sub8 = lax.broadcasted_iota(jnp.int32, (8, 128), 0)

    def turned(v, idx):
        return jnp.take_along_axis(v, idx, axis=1, mode="promise_in_bounds")

    edge = jnp.zeros((8, 128), jnp.float32)
    for d in range(1, G + 1):
        edge = jnp.where(sub8 == d - 1, bm[pl.ds(G + R - d, 1), :], edge)
    send_n[pl.ds(0, 8), :] = turned(edge, turn8)
    send_s[pl.ds(0, 8), :] = bm[pl.ds(G, 8), :]
    for d in range(1, G + 1):
        for f in range(4):
            at = HEAD + (d - 1) * 100 + f * K
            v = turned(m_st[0, f, pl.ds((G + R - d) * K, 32), :], turn32)
            if f >= 2:
                v = v * sign
            send_n[pl.ds(at, K), :] = v[:K]
            send_s[pl.ds(at, K), :] = m_st[0, f, pl.ds((G + d - 1) * K, K), :]

    pl.semaphore_wait(barrier, jnp.where(has_south, 4, 3))

    def remote(src, dst, ss, rs, to):
        return pltpu.make_async_remote_copy(
            src_ref=src, dst_ref=dst, send_sem=ss, recv_sem=rs, device_id=to, device_id_type=mesh_id
        )

    to_east = remote(pack, pack_w, lon_ss.at[0], lon_rs.at[0], {LON: east, LAT: j})
    to_west = remote(pack, pack_e, lon_ss.at[1], lon_rs.at[1], {LON: west, LAT: j})
    to_east.start()
    to_west.start()

    def row_pieces(q):
        if q < G:
            sl = pl.ds(*CHUNKS[q])
            return send_n.at[sl], send_s.at[sl], recv_n.at[sl], recv_s.at[sl]
        return csend_n, csend_s, crecv_n, crecv_s

    def start_rows(q):
        sn, ss, rn, rs = row_pieces(q)

        @pl.when(jnp.logical_not(top))
        def _():
            remote(sn, rs, n_ss.at[q], s_rs.at[q], north).start()

        @pl.when(top)
        def _():
            remote(sn, rn, n_ss.at[q], n_rs.at[q], north).start()

        @pl.when(has_south)
        def _():
            remote(ss, rn, s_ss.at[q], n_rs.at[q], south).start()

    def wait_rows(q):
        sn, ss, rn, rs = row_pieces(q)
        remote(ss, rn, s_ss.at[q], n_rs.at[q], north).wait_recv()

        @pl.when(has_south)
        def _():
            remote(sn, rs, n_ss.at[q], s_rs.at[q], south).wait_recv()

    def wait_sent(q):
        sn, ss, rn, rs = row_pieces(q)
        remote(sn, rs, n_ss.at[q], s_rs.at[q], north).wait_send()

        @pl.when(has_south)
        def _():
            remote(ss, rn, s_ss.at[q], n_rs.at[q], south).wait_send()

    start_rows(0)
    start_rows(1)

    @pl.when(jnp.logical_not(has_south))
    def _():
        zero = jnp.zeros((G * K, 128), jnp.float32)
        bm[pl.ds(0, G), :] = zero[:G]
        bq[pl.ds(0, G), :] = zero[:G]
        for f in range(4):
            m_st[0, f, pl.ds(0, G * K), :] = zero
            q_st[0, f, pl.ds(0, G * K), :] = zero

    to_east.wait_recv()
    to_west.wait_recv()
    west_half = lanes8 % 8 < 4
    for q in range(PACKED // 8):
        both = jnp.where(west_half, pack_w[pl.ds(8 * q, 8), :], pack_e[pl.ds(8 * q, 8), :])
        for g in range(16):
            n = 16 * q + g
            if n >= len(tiles):
                break
            f, k, h = tiles[n]
            v = pltpu.roll(both, (124 - 8 * g) % 128, 1)
            if f < 4:
                q_st[0, f, pl.ds((G + 8 * h) * K + k, 8, stride=K), :] = v
            else:
                bq[pl.ds(G + 8 * h, 8), :] = v

    flip8 = jnp.where(top, lanes8 + 7 - 2 * (lanes8 % 8), lanes8)
    sign8 = jnp.where(lanes8 >= 64, sign, 1.0)
    for d in range(1, G):
        acc_n = acc_s = None
        for g in range(16):
            f, kb = g // 4, KB[g % 4]
            vn = pltpu.roll(q_st[0, f, pl.ds((G + R - d) * K + kb, 8), :], 4 + 8 * g, 1)
            vs = pltpu.roll(q_st[0, f, pl.ds((G + d - 1) * K + kb, 8), :], 4 + 8 * g, 1)
            acc_n = vn if g == 0 else jnp.where(group8 == g, vn, acc_n)
            acc_s = vs if g == 0 else jnp.where(group8 == g, vs, acc_s)
        csend_n[pl.ds(8 * (d - 1), 8), :] = turned(acc_n, flip8) * sign8
        csend_s[pl.ds(8 * (d - 1), 8), :] = acc_s
    edge = jnp.zeros((8, 128), jnp.float32)
    for d in range(1, G + 1):
        edge = jnp.where(sub8 == d - 1, bq[pl.ds(G + R - d, 1), :], edge)
    csend_n[pl.ds(24, 8), :] = turned(pltpu.roll(edge, 4, 1), flip8)
    csend_s[pl.ds(24, 8), :] = pltpu.roll(bq[pl.ds(G, 8), :], 4, 1)
    start_rows(4)
    start_rows(2)
    start_rows(3)

    kk = lax.broadcasted_iota(jnp.int32, (32, 128), 0).astype(jnp.float32)
    first1 = lane((1, 128)) == 0
    last1 = lane((1, 128)) == 127
    firstb = lane((BLOCK, 128)) == 0
    lastb = lane((BLOCK, 128)) == 127
    total_rows = n_lat * R

    def masks(r):
        at = r * K
        bmc, bqc = bm[pl.ds(r, 1), :], bq[pl.ds(r, 1), :]
        me, mw = pltpu.roll(bmc, 127, 1), pltpu.roll(bmc, 1, 1)
        qe, qw = pltpu.roll(bqc, 127, 1), pltpu.roll(bqc, 1, 1)
        sides = (
            (mk, bmc, jnp.where(last1, qe, me), jnp.where(first1, qw, mw), bm),
            (qk, bqc, jnp.where(last1, me, qe), jnp.where(first1, mw, qw), bq),
        )
        for store, c, e, w, rows in sides:
            n, s = rows[pl.ds(r + 1, 1), :], rows[pl.ds(r - 1, 1), :]

            def flag(x):
                return jnp.where(kk < x, 1.0, 0.0)

            wet = flag(c)
            vu = jnp.where(kk >= 1.0, vertical_mixing * wet, 0.0)
            vd = vertical_mixing * flag(c - 1.0)
            drag = jnp.where(kk == c - 1.0, 1.0 - drag_rate, 1.0)
            for q, x in enumerate(
                (
                    flag(jnp.minimum(c, e)), flag(jnp.minimum(c, w)), flag(jnp.minimum(c, n)), flag(jnp.minimum(c, s)),
                    vu, vd, wet - vu - vd, wet * drag,
                )
            ):
                store[q, pl.ds(at, K), :] = x[:K]
        row = j * R + r - G
        row = jnp.where(row >= total_rows, 2 * total_rows - 1 - row, row)
        f = rotation * (2.0 * (row.astype(jnp.float32) + 0.5) / total_rows - 1.0)
        cor[pl.ds(at, K), :] = jnp.full((K, 128), 1.0, jnp.float32) * f

    def pressure(s, start, count, stride):
        for st, out in ((m_st, pm), (q_st, pq)):
            total = None
            for k in range(K):
                sl = pl.ds(start + k, count, stride=stride)
                x = density(st[s, 0, sl, :], st[s, 1, sl, :])
                total = x if total is None else total + x
                out[s, sl, :] = total

    def update(s, b, size, with_q, keep):
        first, last = firstb[:size], lastb[:size]
        sl = pl.ds(b, size)
        mc = [m_st[s, f, sl, :] for f in range(4)] + [pm[s, sl, :]]
        qc = [q_st[s, f, sl, :] for f in range(4)] + [pq[s, sl, :]]
        m_e, m_w, q_e, q_w = [], [], [], []
        for m, q in zip(mc, qc):
            me, mw = pltpu.roll(m, 127, 1), pltpu.roll(m, 1, 1)
            qe, qw = pltpu.roll(q, 127, 1), pltpu.roll(q, 1, 1)
            m_e.append(jnp.where(last, qe, me))
            m_w.append(jnp.where(first, qw, mw))
            if with_q:
                q_e.append(jnp.where(last, me, qe))
                q_w.append(jnp.where(first, mw, qw))
        work = [(m_st, pm, mk, mc, m_e, m_w)]
        if with_q:
            work.append((q_st, pq, qk, qc, q_e, q_w))
        for st, pr, mask, c, e, w in work:
            fe, fw, fn, fs, vu, vd, w0, wd = [mask[q, sl, :] for q in range(N_MASK)]
            a, b_ = courant * c[2], courant * c[3]
            a_neg, b_neg = jnp.minimum(a, 0.0), jnp.minimum(b_, 0.0)
            ce = fe * (mixing - a_neg)
            cw = fw * (mixing + (a - a_neg))
            cn = fn * (mixing - b_neg)
            cs = fs * (mixing + (b_ - b_neg))
            c0 = w0 - ((ce + cw) + (cn + cs))
            north_sl, south_sl = pl.ds(b + K, size), pl.ds(b - K, size)
            new = []
            for f in range(4):
                x = (c0 * c[f] + ce * e[f]) + (cw * w[f] + cn * st[s, f, north_sl, :])
                x = x + (cs * st[s, f, south_sl, :] + vu * st[s, f, pl.ds(b - 1, size), :])
                new.append(x + vd * st[s, f, pl.ds(b + 1, size), :])
            p = c[4]
            px = fe * (e[4] - p) + fw * (p - w[4])
            py = fn * (pr[s, north_sl, :] - p) + fs * (p - pr[s, south_sl, :])
            f0 = cor[sl, :]
            new[2] = wd * (new[2] + f0 * c[3] - px)
            new[3] = wd * (new[3] - f0 * c[2] - py)
            for f in range(4):
                if s < SWEEPS - 1:
                    st[s + 1, f, pl.ds(b, keep), :] = new[f][:keep]
                else:
                    m4[f, pl.ds(b - G * K, keep), :] = new[f][:keep]

    def mask_loop(lo, hi):
        def body(r, carry):
            masks(r)
            return carry

        lax.fori_loop(lo, hi, body, 0)

    mask_loop(G + 1, G + R - 1)
    for s in range(SWEEPS):
        count = R - 2 * s
        pressure(s, (G + s) * K, 8, K)
        pressure(s, (G + R - s - 8) * K, 8, K)
        lo, hi = (G + s + 1) * K, (G + R - s - 1) * K
        steps = -(-(hi - lo) // BLOCK)

        def body(t, carry, s=s, lo=lo, hi=hi):
            b = jnp.minimum(lo + t * BLOCK, hi - BLOCK)
            update(s, b, BLOCK, s < SWEEPS - 1, BLOCK)
            return carry

        lax.fori_loop(0, steps, body, 0)

    def unpack_rows(d):
        for f in range(4):
            src = pl.ds(HEAD + (d - 1) * 100 + f * K, K)
            m_st[0, f, pl.ds((G + R - 1 + d) * K, K), :] = recv_n[src, :]

        @pl.when(has_south)
        def _():
            for f in range(4):
                src = pl.ds(HEAD + (d - 1) * 100 + f * K, K)
                m_st[0, f, pl.ds((G - d) * K, K), :] = recv_s[src, :]

    def unpack_corner(src, row_of):
        edge = pltpu.roll(src[pl.ds(24, 8), :], 124, 1)
        for d in range(1, G + 1):
            bq[pl.ds(row_of(d), 1), :] = edge[d - 1 : d]
        for d in range(1, G):
            both = src[pl.ds(8 * (d - 1), 8), :]
            for g in range(16):
                f, kb = g // 4, KB[g % 4]
                q_st[0, f, pl.ds(row_of(d) * K + kb, 8), :] = pltpu.roll(both, (124 - 8 * g) % 128, 1)

    def north_row(d):
        return G + R - 1 + d

    def south_row(d):
        return G - d

    for e in range(1, G + 1):
        wait_rows(e - 1)
        unpack_rows(e)
        if e == 1:
            wait_rows(4)
            for d in range(1, G + 1):
                bm[pl.ds(north_row(d), 1), :] = recv_n[pl.ds(d - 1, 1), :]
            unpack_corner(crecv_n, north_row)

            @pl.when(has_south)
            def _():
                for d in range(1, G + 1):
                    bm[pl.ds(south_row(d), 1), :] = recv_s[pl.ds(d - 1, 1), :]
                unpack_corner(crecv_s, south_row)

            mask_loop(1, G + 1)
            mask_loop(G + R - 1, 2 * G + R - 1)
        for s in range(SWEEPS):
            d = e - s
            pressure(s, south_row(d) * K, 2, (north_row(d) - south_row(d)) * K)
            for row in (south_row(d - 1), north_row(d - 1)):
                update(s, row * K, 32, s < SWEEPS - 1 and e < G, K)

    done = pltpu.make_async_copy(m4, out_hbm, out_sem.at[0])
    done.start()
    to_east.wait_send()
    to_west.wait_send()
    for q in range(G + 1):
        wait_sent(q)
    done.wait()


def write_out(m4, t_out, s_out, u_out, v_out):
    for f, out in enumerate((t_out, s_out, u_out, v_out)):
        for k in range(K):
            for h in range(2):
                out[k, pl.ds(8 * h, 8), :] = m4[f, pl.ds(8 * h * K + k, 8, stride=K), :]


def per_device(n_lon, n_lat, t, s, u, v, water_indicator, bottom):
    del water_indicator
    f32 = jnp.float32
    hbm = pl.BlockSpec(memory_space=pl.ANY)
    vmem = pltpu.VMEM
    dma = pltpu.SemaphoreType.DMA
    states = pl.pallas_call(
        functools.partial(kernel, n_lon, n_lat),
        out_shape=jax.ShapeDtypeStruct((4, R * K, 128), f32),
        in_specs=[hbm] * 5,
        out_specs=hbm,
        scratch_shapes=[
            vmem((4, K, R, 128), f32), vmem((R, 128), jnp.int32),
            vmem((SWEEPS, 4, LIN, 128), f32), vmem((SWEEPS, 4, LIN, 128), f32), vmem((4, R * K, 128), f32),
            vmem((SWEEPS, LIN, 128), f32), vmem((SWEEPS, LIN, 128), f32),
            vmem((N_MASK, LIN, 128), f32), vmem((N_MASK, LIN, 128), f32), vmem((LIN, 128), f32),
            vmem((32, 128), f32), vmem((32, 128), f32),
            vmem((PACKED, 128), f32), vmem((PACKED, 128), f32), vmem((PACKED, 128), f32),
            vmem((MSG, 128), f32), vmem((MSG, 128), f32), vmem((MSG, 128), f32), vmem((MSG, 128), f32),
            vmem((CORNER, 128), f32), vmem((CORNER, 128), f32), vmem((CORNER, 128), f32), vmem((CORNER, 128), f32),
            dma((5,)), dma((1,)), dma((2,)), dma((2,)), dma((5,)), dma((5,)), dma((5,)), dma((5,)),
        ],
        compiler_params=pltpu.CompilerParams(
            collective_id=1, has_side_effects=True, vmem_limit_bytes=48 * 1024 * 1024
        ),
        name="sweeps",
    )(t, s, u, v, bottom)
    field = jax.ShapeDtypeStruct((K, R, 128), f32)
    return tuple(
        pl.pallas_call(
            write_out,
            out_shape=[field] * 4,
            compiler_params=pltpu.CompilerParams(vmem_limit_bytes=16 * 1024 * 1024),
            name="write_out",
        )(states)
    )


def solution(mesh):
    field = P(None, LAT, LON)
    return jax.shard_map(
        functools.partial(per_device, mesh.shape[LON], mesh.shape[LAT]),
        mesh=mesh,
        in_specs=(field,) * 5 + (P(LAT, LON),),
        out_specs=(field,) * 4,
        check_vma=False,
    )
```

```python
import functools

import jax
import jax.numpy as jnp
from jax import lax
from jax.experimental import pallas as pl
from jax.experimental.pallas import tpu as pltpu
from jax.sharding import PartitionSpec as P

SWEEPS = 4

courant = 0.3
mixing = 0.08
vertical_mixing = 0.1
buoyancy = 0.05
rotation = 0.2
drag_rate = 0.3
thermal = 0.25
haline = 0.2
cabbeling = 0.03

K = 25
R = 16
G = 4
LIN = (R + 2 * G) * K + 16
BLOCK = 56
HEAD = 8
CHUNKS = ((0, 112), (112, 96), (208, 104), (312, 96))
MSG = 408
PACKED = 104
CORNER = 32
KB = (0, 8, 16, 17)
N_MASK = 8

LON, LAT = "lon", "lat"


def lane(shape):
    return lax.broadcasted_iota(jnp.int32, shape, 1)


def density(t, s):
    h = 0.5 * buoyancy
    return t * (-thermal * h - (cabbeling * h) * t) + (haline * h) * s


def kernel(
    n_lon, n_lat, t_hbm, s_hbm, u_hbm, v_hbm, b_hbm, m4,
    xin, bin_, m_st, q_st, pm, pq, mk, qk, cor, bm, bq,
    pack, pack_w, pack_e, send_n, send_s, recv_n, recv_s, csend_n, csend_s, crecv_n, crecv_s,
    in_sem, lon_ss, lon_rs, n_ss, n_rs, s_ss, s_rs,
):
    i = lax.axis_index(LON)
    j = lax.axis_index(LAT)
    top = j == n_lat - 1
    east = lax.rem(i + 1, n_lon)
    west = lax.rem(i + n_lon - 1, n_lon)
    has_south = j > 0
    north = {LON: jnp.where(top, n_lon - 1 - i, i), LAT: jnp.where(top, j, j + 1)}
    south = {LON: i, LAT: jnp.maximum(j - 1, 0)}
    mesh_id = pl.DeviceIdType.MESH

    barrier = pltpu.get_barrier_semaphore()
    pl.semaphore_signal(barrier, inc=1, device_id={LON: east, LAT: j}, device_id_type=mesh_id)
    pl.semaphore_signal(barrier, inc=1, device_id={LON: west, LAT: j}, device_id_type=mesh_id)
    pl.semaphore_signal(barrier, inc=1, device_id=north, device_id_type=mesh_id)

    @pl.when(has_south)
    def _():
        pl.semaphore_signal(barrier, inc=1, device_id=south, device_id_type=mesh_id)

    loads = [
        pltpu.make_async_copy(ref, xin.at[f], in_sem.at[f])
        for f, ref in enumerate((t_hbm, s_hbm, u_hbm, v_hbm))
    ]
    loads.append(pltpu.make_async_copy(b_hbm, bin_, in_sem.at[4]))
    for c in loads:
        c.start()
    for c in loads:
        c.wait()

    lanes8 = lane((8, 128))
    group8 = lanes8 // 8

    bm[pl.ds(G, R), :] = bin_[...].astype(jnp.float32)
    tiles = [(f, k, h) for f in range(4) for k in range(K) for h in range(2)]
    tiles += [(4, 0, 0), (4, 0, 1)]
    acc = None
    for n, (f, k, h) in enumerate(tiles):
        if f < 4:
            v = xin[f, k, pl.ds(8 * h, 8), :]
            m_st[0, f, pl.ds((G + 8 * h) * K + k, 8, stride=K), :] = v
        else:
            v = bm[pl.ds(G + 8 * h, 8), :]
        g = n % 16
        rolled = pltpu.roll(v, 4 + 8 * g, 1)
        acc = rolled if g == 0 else jnp.where(group8 == g, rolled, acc)
        if g == 15 or n == len(tiles) - 1:
            pack[pl.ds(8 * (n // 16), 8), :] = acc

    sign = jnp.where(top, -1.0, 1.0).astype(jnp.float32)
    lanes32 = lane((32, 128))
    turn32 = jnp.where(top, 127 - lanes32, lanes32)
    turn8 = jnp.where(top, 127 - lanes8, lanes8)
    sub8 = lax.broadcasted_iota(jnp.int32, (8, 128), 0)

    def turned(v, idx):
        return jnp.take_along_axis(v, idx, axis=1, mode="promise_in_bounds")

    edge = jnp.zeros((8, 128), jnp.float32)
    for d in range(1, G + 1):
        edge = jnp.where(sub8 == d - 1, bm[pl.ds(G + R - d, 1), :], edge)
    send_n[pl.ds(0, 8), :] = turned(edge, turn8)
    send_s[pl.ds(0, 8), :] = bm[pl.ds(G, 8), :]
    for d in range(1, G + 1):
        for f in range(4):
            at = HEAD + (d - 1) * 100 + f * K
            v = turned(m_st[0, f, pl.ds((G + R - d) * K, 32), :], turn32)
            if f >= 2:
                v = v * sign
            send_n[pl.ds(at, K), :] = v[:K]
            send_s[pl.ds(at, K), :] = m_st[0, f, pl.ds((G + d - 1) * K, K), :]

    pl.semaphore_wait(barrier, jnp.where(has_south, 4, 3))

    def remote(src, dst, ss, rs, to):
        return pltpu.make_async_remote_copy(
            src_ref=src, dst_ref=dst, send_sem=ss, recv_sem=rs, device_id=to, device_id_type=mesh_id
        )

    to_east = remote(pack, pack_w, lon_ss.at[0], lon_rs.at[0], {LON: east, LAT: j})
    to_west = remote(pack, pack_e, lon_ss.at[1], lon_rs.at[1], {LON: west, LAT: j})
    to_east.start()
    to_west.start()

    def row_pieces(q):
        if q < G:
            sl = pl.ds(*CHUNKS[q])
            return send_n.at[sl], send_s.at[sl], recv_n.at[sl], recv_s.at[sl]
        return csend_n, csend_s, crecv_n, crecv_s

    def start_rows(q):
        sn, ss, rn, rs = row_pieces(q)

        @pl.when(jnp.logical_not(top))
        def _():
            remote(sn, rs, n_ss.at[q], s_rs.at[q], north).start()

        @pl.when(top)
        def _():
            remote(sn, rn, n_ss.at[q], n_rs.at[q], north).start()

        @pl.when(has_south)
        def _():
            remote(ss, rn, s_ss.at[q], n_rs.at[q], south).start()

    def wait_rows(q):
        sn, ss, rn, rs = row_pieces(q)
        remote(ss, rn, s_ss.at[q], n_rs.at[q], north).wait_recv()

        @pl.when(has_south)
        def _():
            remote(sn, rs, n_ss.at[q], s_rs.at[q], south).wait_recv()

    def wait_sent(q):
        sn, ss, rn, rs = row_pieces(q)
        remote(sn, rs, n_ss.at[q], s_rs.at[q], north).wait_send()

        @pl.when(has_south)
        def _():
            remote(ss, rn, s_ss.at[q], n_rs.at[q], south).wait_send()

    start_rows(0)
    start_rows(1)

    @pl.when(jnp.logical_not(has_south))
    def _():
        zero = jnp.zeros((G * K, 128), jnp.float32)
        bm[pl.ds(0, G), :] = zero[:G]
        bq[pl.ds(0, G), :] = zero[:G]
        for f in range(4):
            m_st[0, f, pl.ds(0, G * K), :] = zero
            q_st[0, f, pl.ds(0, G * K), :] = zero

    to_east.wait_recv()
    to_west.wait_recv()
    west_half = lanes8 % 8 < 4
    for q in range(PACKED // 8):
        both = jnp.where(west_half, pack_w[pl.ds(8 * q, 8), :], pack_e[pl.ds(8 * q, 8), :])
        for g in range(16):
            n = 16 * q + g
            if n >= len(tiles):
                break
            f, k, h = tiles[n]
            v = pltpu.roll(both, (124 - 8 * g) % 128, 1)
            if f < 4:
                q_st[0, f, pl.ds((G + 8 * h) * K + k, 8, stride=K), :] = v
            else:
                bq[pl.ds(G + 8 * h, 8), :] = v

    flip8 = jnp.where(top, lanes8 + 7 - 2 * (lanes8 % 8), lanes8)
    sign8 = jnp.where(lanes8 >= 64, sign, 1.0)
    for d in range(1, G):
        acc_n = acc_s = None
        for g in range(16):
            f, kb = g // 4, KB[g % 4]
            vn = pltpu.roll(q_st[0, f, pl.ds((G + R - d) * K + kb, 8), :], 4 + 8 * g, 1)
            vs = pltpu.roll(q_st[0, f, pl.ds((G + d - 1) * K + kb, 8), :], 4 + 8 * g, 1)
            acc_n = vn if g == 0 else jnp.where(group8 == g, vn, acc_n)
            acc_s = vs if g == 0 else jnp.where(group8 == g, vs, acc_s)
        csend_n[pl.ds(8 * (d - 1), 8), :] = turned(acc_n, flip8) * sign8
        csend_s[pl.ds(8 * (d - 1), 8), :] = acc_s
    edge = jnp.zeros((8, 128), jnp.float32)
    for d in range(1, G + 1):
        edge = jnp.where(sub8 == d - 1, bq[pl.ds(G + R - d, 1), :], edge)
    csend_n[pl.ds(24, 8), :] = turned(pltpu.roll(edge, 4, 1), flip8)
    csend_s[pl.ds(24, 8), :] = pltpu.roll(bq[pl.ds(G, 8), :], 4, 1)
    start_rows(4)
    start_rows(2)
    start_rows(3)

    kk = lax.broadcasted_iota(jnp.int32, (32, 128), 0).astype(jnp.float32)
    first1 = lane((1, 128)) == 0
    last1 = lane((1, 128)) == 127
    firstb = lane((BLOCK, 128)) == 0
    lastb = lane((BLOCK, 128)) == 127
    total_rows = n_lat * R

    def masks(r):
        at = r * K
        bmc, bqc = bm[pl.ds(r, 1), :], bq[pl.ds(r, 1), :]
        me, mw = pltpu.roll(bmc, 127, 1), pltpu.roll(bmc, 1, 1)
        qe, qw = pltpu.roll(bqc, 127, 1), pltpu.roll(bqc, 1, 1)
        sides = (
            (mk, bmc, jnp.where(last1, qe, me), jnp.where(first1, qw, mw), bm),
            (qk, bqc, jnp.where(last1, me, qe), jnp.where(first1, mw, qw), bq),
        )
        for store, c, e, w, rows in sides:
            n, s = rows[pl.ds(r + 1, 1), :], rows[pl.ds(r - 1, 1), :]

            def flag(x):
                return jnp.where(kk < x, 1.0, 0.0)

            wet = flag(c)
            vu = jnp.where(kk >= 1.0, vertical_mixing * wet, 0.0)
            vd = vertical_mixing * flag(c - 1.0)
            drag = jnp.where(kk == c - 1.0, 1.0 - drag_rate, 1.0)
            for q, x in enumerate(
                (
                    flag(jnp.minimum(c, e)), flag(jnp.minimum(c, w)), flag(jnp.minimum(c, n)), flag(jnp.minimum(c, s)),
                    vu, vd, wet - vu - vd, wet * drag,
                )
            ):
                store[q, pl.ds(at, K), :] = x[:K]
        row = j * R + r - G
        row = jnp.where(row >= total_rows, 2 * total_rows - 1 - row, row)
        f = rotation * (2.0 * (row.astype(jnp.float32) + 0.5) / total_rows - 1.0)
        cor[pl.ds(at, K), :] = jnp.full((K, 128), 1.0, jnp.float32) * f

    def pressure(s, start, count, stride):
        for st, out in ((m_st, pm), (q_st, pq)):
            total = None
            for k in range(K):
                sl = pl.ds(start + k, count, stride=stride)
                x = density(st[s, 0, sl, :], st[s, 1, sl, :])
                total = x if total is None else total + x
                out[s, sl, :] = total

    def update(s, b, size, with_q, keep):
        first, last = firstb[:size], lastb[:size]
        sl = pl.ds(b, size)
        mc = [m_st[s, f, sl, :] for f in range(4)] + [pm[s, sl, :]]
        qc = [q_st[s, f, sl, :] for f in range(4)] + [pq[s, sl, :]]
        m_e, m_w, q_e, q_w = [], [], [], []
        for m, q in zip(mc, qc):
            me, mw = pltpu.roll(m, 127, 1), pltpu.roll(m, 1, 1)
            qe, qw = pltpu.roll(q, 127, 1), pltpu.roll(q, 1, 1)
            m_e.append(jnp.where(last, qe, me))
            m_w.append(jnp.where(first, qw, mw))
            if with_q:
                q_e.append(jnp.where(last, me, qe))
                q_w.append(jnp.where(first, mw, qw))
        work = [(m_st, pm, mk, mc, m_e, m_w)]
        if with_q:
            work.append((q_st, pq, qk, qc, q_e, q_w))
        for st, pr, mask, c, e, w in work:
            fe, fw, fn, fs, vu, vd, w0, wd = [mask[q, sl, :] for q in range(N_MASK)]
            a, b_ = courant * c[2], courant * c[3]
            a_neg, b_neg = jnp.minimum(a, 0.0), jnp.minimum(b_, 0.0)
            ce = fe * (mixing - a_neg)
            cw = fw * (mixing + (a - a_neg))
            cn = fn * (mixing - b_neg)
            cs = fs * (mixing + (b_ - b_neg))
            c0 = w0 - ((ce + cw) + (cn + cs))
            north_sl, south_sl = pl.ds(b + K, size), pl.ds(b - K, size)
            new = []
            for f in range(4):
                x = (c0 * c[f] + ce * e[f]) + (cw * w[f] + cn * st[s, f, north_sl, :])
                x = x + (cs * st[s, f, south_sl, :] + vu * st[s, f, pl.ds(b - 1, size), :])
                new.append(x + vd * st[s, f, pl.ds(b + 1, size), :])
            p = c[4]
            px = fe * (e[4] - p) + fw * (p - w[4])
            py = fn * (pr[s, north_sl, :] - p) + fs * (p - pr[s, south_sl, :])
            f0 = cor[sl, :]
            new[2] = wd * (new[2] + f0 * c[3] - px)
            new[3] = wd * (new[3] - f0 * c[2] - py)
            for f in range(4):
                if s < SWEEPS - 1:
                    st[s + 1, f, pl.ds(b, keep), :] = new[f][:keep]
                else:
                    m4[f, pl.ds(b - G * K, keep), :] = new[f][:keep]

    def mask_loop(lo, hi):
        def body(r, carry):
            masks(r)
            return carry

        lax.fori_loop(lo, hi, body, 0)

    mask_loop(G + 1, G + R - 1)
    for s in range(SWEEPS):
        count = R - 2 * s
        pressure(s, (G + s) * K, 8, K)
        pressure(s, (G + R - s - 8) * K, 8, K)
        lo, hi = (G + s + 1) * K, (G + R - s - 1) * K
        steps = -(-(hi - lo) // BLOCK)

        def body(t, carry, s=s, lo=lo, hi=hi):
            b = jnp.minimum(lo + t * BLOCK, hi - BLOCK)
            update(s, b, BLOCK, s < SWEEPS - 1, BLOCK)
            return carry

        lax.fori_loop(0, steps, body, 0)

    def unpack_rows(d):
        for f in range(4):
            src = pl.ds(HEAD + (d - 1) * 100 + f * K, K)
            m_st[0, f, pl.ds((G + R - 1 + d) * K, K), :] = recv_n[src, :]

        @pl.when(has_south)
        def _():
            for f in range(4):
                src = pl.ds(HEAD + (d - 1) * 100 + f * K, K)
                m_st[0, f, pl.ds((G - d) * K, K), :] = recv_s[src, :]

    def unpack_corner(src, row_of):
        edge = pltpu.roll(src[pl.ds(24, 8), :], 124, 1)
        for d in range(1, G + 1):
            bq[pl.ds(row_of(d), 1), :] = edge[d - 1 : d]
        for d in range(1, G):
            both = src[pl.ds(8 * (d - 1), 8), :]
            for g in range(16):
                f, kb = g // 4, KB[g % 4]
                q_st[0, f, pl.ds(row_of(d) * K + kb, 8), :] = pltpu.roll(both, (124 - 8 * g) % 128, 1)

    def north_row(d):
        return G + R - 1 + d

    def south_row(d):
        return G - d

    for e in range(1, G + 1):
        wait_rows(e - 1)
        unpack_rows(e)
        if e == 1:
            wait_rows(4)
            for d in range(1, G + 1):
                bm[pl.ds(north_row(d), 1), :] = recv_n[pl.ds(d - 1, 1), :]
            unpack_corner(crecv_n, north_row)

            @pl.when(has_south)
            def _():
                for d in range(1, G + 1):
                    bm[pl.ds(south_row(d), 1), :] = recv_s[pl.ds(d - 1, 1), :]
                unpack_corner(crecv_s, south_row)

            mask_loop(1, G + 1)
            mask_loop(G + R - 1, 2 * G + R - 1)
        for s in range(SWEEPS):
            d = e - s
            pressure(s, south_row(d) * K, 2, (north_row(d) - south_row(d)) * K)
            for row in (south_row(d - 1), north_row(d - 1)):
                update(s, row * K, 32, s < SWEEPS - 1 and e < G, K)

    to_east.wait_send()
    to_west.wait_send()
    for q in range(G + 1):
        wait_sent(q)


def write_out(m4, t_out, s_out, u_out, v_out):
    for f, out in enumerate((t_out, s_out, u_out, v_out)):
        for k in range(K):
            for h in range(2):
                out[k, pl.ds(8 * h, 8), :] = m4[f, pl.ds(8 * h * K + k, 8, stride=K), :]


def per_device(n_lon, n_lat, t, s, u, v, water_indicator, bottom):
    del water_indicator
    f32 = jnp.float32
    hbm = pl.BlockSpec(memory_space=pl.ANY)
    vmem = pltpu.VMEM
    dma = pltpu.SemaphoreType.DMA
    states = pl.pallas_call(
        functools.partial(kernel, n_lon, n_lat),
        out_shape=pltpu.VMEM((4, R * K, 128), f32),
        in_specs=[hbm] * 5,
        out_specs=pl.BlockSpec(memory_space=pltpu.VMEM),
        scratch_shapes=[
            vmem((4, K, R, 128), f32), vmem((R, 128), jnp.int32),
            vmem((SWEEPS, 4, LIN, 128), f32), vmem((SWEEPS, 4, LIN, 128), f32),
            vmem((SWEEPS, LIN, 128), f32), vmem((SWEEPS, LIN, 128), f32),
            vmem((N_MASK, LIN, 128), f32), vmem((N_MASK, LIN, 128), f32), vmem((LIN, 128), f32),
            vmem((32, 128), f32), vmem((32, 128), f32),
            vmem((PACKED, 128), f32), vmem((PACKED, 128), f32), vmem((PACKED, 128), f32),
            vmem((MSG, 128), f32), vmem((MSG, 128), f32), vmem((MSG, 128), f32), vmem((MSG, 128), f32),
            vmem((CORNER, 128), f32), vmem((CORNER, 128), f32), vmem((CORNER, 128), f32), vmem((CORNER, 128), f32),
            dma((5,)), dma((2,)), dma((2,)), dma((5,)), dma((5,)), dma((5,)), dma((5,)),
        ],
        compiler_params=pltpu.CompilerParams(
            collective_id=1, has_side_effects=True, vmem_limit_bytes=48 * 1024 * 1024
        ),
        name="sweeps",
    )(*(pltpu.with_memory_space_constraint(x, pltpu.HBM) for x in (t, s, u, v, bottom)))
    field = jax.ShapeDtypeStruct((K, R, 128), f32)
    return tuple(
        pl.pallas_call(
            write_out,
            out_shape=[field] * 4,
            compiler_params=pltpu.CompilerParams(vmem_limit_bytes=16 * 1024 * 1024),
            name="write_out",
        )(states)
    )


def solution(mesh):
    field = P(None, LAT, LON)
    return jax.shard_map(
        functools.partial(per_device, mesh.shape[LON], mesh.shape[LAT]),
        mesh=mesh,
        in_specs=(field,) * 5 + (P(LAT, LON),),
        out_specs=(field,) * 4,
        check_vma=False,
    )
```

```python
import functools

import jax
import jax.numpy as jnp
from jax import lax
from jax.experimental import pallas as pl
from jax.experimental.pallas import tpu as pltpu
from jax.sharding import PartitionSpec as P

SWEEPS = 4

courant = 0.3
mixing = 0.08
vertical_mixing = 0.1
buoyancy = 0.05
rotation = 0.2
drag_rate = 0.3
thermal = 0.25
haline = 0.2
cabbeling = 0.03

K = 25
R = 16
G = 4
LIN = (R + 2 * G) * K + 16
BLOCK = 56
HEAD = 8
CHUNKS = ((0, 112), (112, 96), (208, 104), (312, 96))
MSG = 408
PACKED = 104
CORNER = 32
KB = (0, 8, 16, 17)
N_MASK = 8

LON, LAT = "lon", "lat"


def lane(shape):
    return lax.broadcasted_iota(jnp.int32, shape, 1)


def density(t, s):
    h = 0.5 * buoyancy
    return t * (-thermal * h - (cabbeling * h) * t) + (haline * h) * s


def kernel(
    n_lon, n_lat, t_hbm, s_hbm, u_hbm, v_hbm, b_hbm, m4,
    xin, bin_, m_st, q_st, pm, pq, mk, qk, cor, bm, bq, b_side,
    pack, pack_w, pack_e, send_n, send_s, recv_n, recv_s, passing, csend_n, csend_s, crecv_n, crecv_s,
    in_sem, lon_ss, lon_rs, n_ss, n_rs, s_ss, s_rs, pass_ss, pass_rs,
):
    i = lax.axis_index(LON)
    j = lax.axis_index(LAT)
    top = j == n_lat - 1
    east = lax.rem(i + 1, n_lon)
    west = lax.rem(i + n_lon - 1, n_lon)
    has_south = j > 0
    north = {LON: jnp.where(top, n_lon - 1 - i, i), LAT: jnp.where(top, j, j + 1)}
    south = {LON: i, LAT: jnp.maximum(j - 1, 0)}
    mesh_id = pl.DeviceIdType.MESH
    relays = j == n_lat - 2
    across = lax.rem(i + n_lon // 2, n_lon)
    relay = {LON: across, LAT: jnp.maximum(n_lat - 2, 0)}
    relayed = {LON: across, LAT: n_lat - 1}

    barrier = pltpu.get_barrier_semaphore()
    pl.semaphore_signal(barrier, inc=1, device_id={LON: east, LAT: j}, device_id_type=mesh_id)
    pl.semaphore_signal(barrier, inc=1, device_id={LON: west, LAT: j}, device_id_type=mesh_id)
    pl.semaphore_signal(barrier, inc=1, device_id=north, device_id_type=mesh_id)

    @pl.when(has_south)
    def _():
        pl.semaphore_signal(barrier, inc=1, device_id=south, device_id_type=mesh_id)

    @pl.when(jnp.logical_or(top, relays))
    def _():
        pl.semaphore_signal(barrier, inc=1, device_id=relay, device_id_type=mesh_id)

    @pl.when(relays)
    def _():
        pl.semaphore_signal(barrier, inc=1, device_id=relayed, device_id_type=mesh_id)

    loads = [
        pltpu.make_async_copy(ref, xin.at[f], in_sem.at[f])
        for f, ref in enumerate((t_hbm, s_hbm, u_hbm, v_hbm))
    ]
    loads.append(pltpu.make_async_copy(b_hbm, bin_, in_sem.at[4]))
    for c in loads:
        c.start()
    for c in loads:
        c.wait()

    lanes8 = lane((8, 128))
    group8 = lanes8 // 8

    bm[pl.ds(G, R), :] = bin_[...].astype(jnp.float32)
    tiles = [(f, k, h) for f in range(4) for k in range(K) for h in range(2)]
    tiles += [(4, 0, 0), (4, 0, 1)]
    acc = None
    for n, (f, k, h) in enumerate(tiles):
        if f < 4:
            v = xin[f, k, pl.ds(8 * h, 8), :]
            m_st[0, f, pl.ds((G + 8 * h) * K + k, 8, stride=K), :] = v
        else:
            v = bm[pl.ds(G + 8 * h, 8), :]
        g = n % 16
        rolled = pltpu.roll(v, 4 + 8 * g, 1)
        acc = rolled if g == 0 else jnp.where(group8 == g, rolled, acc)
        if g == 15 or n == len(tiles) - 1:
            pack[pl.ds(8 * (n // 16), 8), :] = acc

    sign = jnp.where(top, -1.0, 1.0).astype(jnp.float32)
    lanes32 = lane((32, 128))
    turn32 = jnp.where(top, 127 - lanes32, lanes32)
    turn8 = jnp.where(top, 127 - lanes8, lanes8)
    sub8 = lax.broadcasted_iota(jnp.int32, (8, 128), 0)

    def turned(v, idx):
        return jnp.take_along_axis(v, idx, axis=1, mode="promise_in_bounds")

    edge = jnp.zeros((8, 128), jnp.float32)
    for d in range(1, G + 1):
        edge = jnp.where(sub8 == d - 1, bm[pl.ds(G + R - d, 1), :], edge)
    send_n[pl.ds(0, 8), :] = turned(edge, turn8)
    send_s[pl.ds(0, 8), :] = bm[pl.ds(G, 8), :]
    for d in range(1, G + 1):
        for f in range(4):
            at = HEAD + (d - 1) * 100 + f * K
            v = turned(m_st[0, f, pl.ds((G + R - d) * K, 32), :], turn32)
            if f >= 2:
                v = v * sign
            send_n[pl.ds(at, K), :] = v[:K]
            send_s[pl.ds(at, K), :] = m_st[0, f, pl.ds((G + d - 1) * K, K), :]

    pl.semaphore_wait(barrier, jnp.where(has_south, 4, 3) + jnp.where(top, 1, 0) + jnp.where(relays, 2, 0))

    def remote(src, dst, ss, rs, to):
        return pltpu.make_async_remote_copy(
            src_ref=src, dst_ref=dst, send_sem=ss, recv_sem=rs, device_id=to, device_id_type=mesh_id
        )

    to_east = remote(pack, pack_w, lon_ss.at[0], lon_rs.at[0], {LON: east, LAT: j})
    to_west = remote(pack, pack_e, lon_ss.at[1], lon_rs.at[1], {LON: west, LAT: j})
    to_east.start()
    to_west.start()

    def row_pieces(q):
        if q < G:
            sl = pl.ds(*CHUNKS[q])
            return send_n.at[sl], send_s.at[sl], recv_n.at[sl], recv_s.at[sl]
        return csend_n, csend_s, crecv_n, crecv_s

    def start_rows(q):
        sn, ss, rn, rs = row_pieces(q)

        @pl.when(jnp.logical_not(top))
        def _():
            remote(sn, rs, n_ss.at[q], s_rs.at[q], north).start()

        @pl.when(top)
        def _():
            remote(sn, rn, n_ss.at[q], n_rs.at[q], north).start()

        direct = has_south if q == G else jnp.logical_and(has_south, jnp.logical_not(top))

        @pl.when(direct)
        def _():
            remote(ss, rn, s_ss.at[q], n_rs.at[q], south).start()

        if q < G:

            @pl.when(top)
            def _():
                remote(ss, passing.at[pl.ds(*CHUNKS[q])], s_ss.at[q], pass_rs.at[q], relay).start()

    def wait_rows(q):
        sn, ss, rn, rs = row_pieces(q)
        remote(ss, rn, s_ss.at[q], n_rs.at[q], north).wait_recv()

        @pl.when(has_south)
        def _():
            remote(sn, rs, n_ss.at[q], s_rs.at[q], south).wait_recv()

    def passed(q):
        sl = pl.ds(*CHUNKS[q])
        return remote(passing.at[sl], recv_n.at[sl], pass_ss.at[q], n_rs.at[q], relay)

    def pass_on(q):
        @pl.when(relays)
        def _():
            sl = pl.ds(*CHUNKS[q])
            remote(send_s.at[sl], passing.at[sl], s_ss.at[q], pass_rs.at[q], relay).wait_recv()
            passed(q).start()

    def wait_sent(q):
        sn, ss, rn, rs = row_pieces(q)
        remote(sn, rs, n_ss.at[q], s_rs.at[q], north).wait_send()

        @pl.when(has_south)
        def _():
            remote(ss, rn, s_ss.at[q], n_rs.at[q], south).wait_send()

    start_rows(0)
    start_rows(1)

    @pl.when(jnp.logical_not(has_south))
    def _():
        zero = jnp.zeros((G * K, 128), jnp.float32)
        bm[pl.ds(0, G), :] = zero[:G]
        bq[pl.ds(0, G), :] = zero[:G]
        for f in range(4):
            m_st[0, f, pl.ds(0, G * K), :] = zero
            q_st[0, f, pl.ds(0, G * K), :] = zero

    to_east.wait_recv()
    to_west.wait_recv()
    west_half = lanes8 % 8 < 4
    for q in range(PACKED // 8):
        both = jnp.where(west_half, pack_w[pl.ds(8 * q, 8), :], pack_e[pl.ds(8 * q, 8), :])
        for g in range(16):
            n = 16 * q + g
            if n >= len(tiles):
                break
            f, k, h = tiles[n]
            v = pltpu.roll(both, (124 - 8 * g) % 128, 1)
            if f < 4:
                q_st[0, f, pl.ds((G + 8 * h) * K + k, 8, stride=K), :] = v
            else:
                bq[pl.ds(G + 8 * h, 8), :] = v

    flip8 = jnp.where(top, lanes8 + 7 - 2 * (lanes8 % 8), lanes8)
    sign8 = jnp.where(lanes8 >= 64, sign, 1.0)
    for d in range(1, G):
        acc_n = acc_s = None
        for g in range(16):
            f, kb = g // 4, KB[g % 4]
            vn = pltpu.roll(q_st[0, f, pl.ds((G + R - d) * K + kb, 8), :], 4 + 8 * g, 1)
            vs = pltpu.roll(q_st[0, f, pl.ds((G + d - 1) * K + kb, 8), :], 4 + 8 * g, 1)
            acc_n = vn if g == 0 else jnp.where(group8 == g, vn, acc_n)
            acc_s = vs if g == 0 else jnp.where(group8 == g, vs, acc_s)
        csend_n[pl.ds(8 * (d - 1), 8), :] = turned(acc_n, flip8) * sign8
        csend_s[pl.ds(8 * (d - 1), 8), :] = acc_s
    edge = jnp.zeros((8, 128), jnp.float32)
    for d in range(1, G + 1):
        edge = jnp.where(sub8 == d - 1, bq[pl.ds(G + R - d, 1), :], edge)
    csend_n[pl.ds(24, 8), :] = turned(pltpu.roll(edge, 4, 1), flip8)
    csend_s[pl.ds(24, 8), :] = pltpu.roll(bq[pl.ds(G, 8), :], 4, 1)
    start_rows(4)
    start_rows(2)
    start_rows(3)
    pass_on(0)
    pass_on(1)

    kk = lax.broadcasted_iota(jnp.int32, (32, 128), 0).astype(jnp.float32)
    firstb = lane((BLOCK, 128)) == 0
    lastb = lane((BLOCK, 128)) == 127
    total_rows = n_lat * R

    def sides_of_bottom(rows):
        for r in rows:
            sl = pl.ds(r, 8)
            m, q = bm[sl, :], bq[sl, :]
            first, last = lanes8 == 0, lanes8 == 127
            b_side[0, sl, :] = pltpu.roll(jnp.where(first, q, m), 127, 1)
            b_side[1, sl, :] = pltpu.roll(jnp.where(last, q, m), 1, 1)
            b_side[2, sl, :] = pltpu.roll(jnp.where(first, m, q), 127, 1)
            b_side[3, sl, :] = pltpu.roll(jnp.where(last, m, q), 1, 1)

    def masks(r):
        at = r * K
        one = pl.ds(r, 1)
        sides = (
            (mk, bm[one, :], b_side[0, one, :], b_side[1, one, :], bm),
            (qk, bq[one, :], b_side[2, one, :], b_side[3, one, :], bq),
        )
        for store, c, e, w, rows in sides:
            n, s = rows[pl.ds(r + 1, 1), :], rows[pl.ds(r - 1, 1), :]

            def flag(x):
                return jnp.where(kk < x, 1.0, 0.0)

            wet = flag(c)
            vu = jnp.where(kk >= 1.0, vertical_mixing * wet, 0.0)
            vd = vertical_mixing * flag(c - 1.0)
            drag = jnp.where(kk == c - 1.0, 1.0 - drag_rate, 1.0)
            for q, x in enumerate(
                (
                    flag(jnp.minimum(c, e)), flag(jnp.minimum(c, w)), flag(jnp.minimum(c, n)), flag(jnp.minimum(c, s)),
                    vu, vd, wet - vu - vd, wet * drag,
                )
            ):
                store[q, pl.ds(at, K), :] = x[:K]
        row = j * R + r - G
        row = jnp.where(row >= total_rows, 2 * total_rows - 1 - row, row)
        f = rotation * (2.0 * (row.astype(jnp.float32) + 0.5) / total_rows - 1.0)
        cor[pl.ds(at, K), :] = jnp.full((K, 128), 1.0, jnp.float32) * f

    def pressure(s, start, count, stride):
        for st, out in ((m_st, pm), (q_st, pq)):
            total = None
            for k in range(K):
                sl = pl.ds(start + k, count, stride=stride)
                x = density(st[s, 0, sl, :], st[s, 1, sl, :])
                total = x if total is None else total + x
                out[s, sl, :] = total

    def update(s, b, size, with_q, keep):
        first, last = firstb[:size], lastb[:size]
        sl = pl.ds(b, size)
        mc = [m_st[s, f, sl, :] for f in range(4)] + [pm[s, sl, :]]
        qc = [q_st[s, f, sl, :] for f in range(4)] + [pq[s, sl, :]]
        m_e, m_w, q_e, q_w = [], [], [], []
        for m, q in zip(mc, qc):
            me, mw = pltpu.roll(m, 127, 1), pltpu.roll(m, 1, 1)
            qe, qw = pltpu.roll(q, 127, 1), pltpu.roll(q, 1, 1)
            m_e.append(jnp.where(last, qe, me))
            m_w.append(jnp.where(first, qw, mw))
            if with_q:
                q_e.append(jnp.where(last, me, qe))
                q_w.append(jnp.where(first, mw, qw))
        work = [(m_st, pm, mk, mc, m_e, m_w)]
        if with_q:
            work.append((q_st, pq, qk, qc, q_e, q_w))
        for st, pr, mask, c, e, w in work:
            fe, fw, fn, fs, vu, vd, w0, wd = [mask[q, sl, :] for q in range(N_MASK)]
            a, b_ = courant * c[2], courant * c[3]
            a_neg, b_neg = jnp.minimum(a, 0.0), jnp.minimum(b_, 0.0)
            ce = fe * (mixing - a_neg)
            cw = fw * (mixing + (a - a_neg))
            cn = fn * (mixing - b_neg)
            cs = fs * (mixing + (b_ - b_neg))
            c0 = w0 - ((ce + cw) + (cn + cs))
            north_sl, south_sl = pl.ds(b + K, size), pl.ds(b - K, size)
            new = []
            for f in range(4):
                x = (c0 * c[f] + ce * e[f]) + (cw * w[f] + cn * st[s, f, north_sl, :])
                x = x + (cs * st[s, f, south_sl, :] + vu * st[s, f, pl.ds(b - 1, size), :])
                new.append(x + vd * st[s, f, pl.ds(b + 1, size), :])
            p = c[4]
            px = fe * (e[4] - p) + fw * (p - w[4])
            py = fn * (pr[s, north_sl, :] - p) + fs * (p - pr[s, south_sl, :])
            f0 = cor[sl, :]
            new[2] = wd * (new[2] + f0 * c[3] - px)
            new[3] = wd * (new[3] - f0 * c[2] - py)
            for f in range(4):
                if s < SWEEPS - 1:
                    st[s + 1, f, pl.ds(b, keep), :] = new[f][:keep]
                else:
                    m4[f, pl.ds(b - G * K, keep), :] = new[f][:keep]

    def mask_loop(lo, hi):
        def body(r, carry):
            masks(r)
            return carry

        lax.fori_loop(lo, hi, body, 0)

    sides_of_bottom((G, G + 8))
    mask_loop(G + 1, G + R - 1)
    for s in range(SWEEPS):
        count = R - 2 * s
        pressure(s, (G + s) * K, 8, K)
        pressure(s, (G + R - s - 8) * K, 8, K)
        lo, hi = (G + s + 1) * K, (G + R - s - 1) * K
        steps = -(-(hi - lo) // BLOCK)

        def body(t, carry, s=s, lo=lo, hi=hi):
            b = jnp.minimum(lo + t * BLOCK, hi - BLOCK)
            update(s, b, BLOCK, s < SWEEPS - 1, BLOCK)
            return carry

        lax.fori_loop(0, steps, body, 0)
        if s in (0, 1):
            pass_on(s + 2)

    def unpack_rows(d):
        for f in range(4):
            src = pl.ds(HEAD + (d - 1) * 100 + f * K, K)
            m_st[0, f, pl.ds((G + R - 1 + d) * K, K), :] = recv_n[src, :]

        @pl.when(has_south)
        def _():
            for f in range(4):
                src = pl.ds(HEAD + (d - 1) * 100 + f * K, K)
                m_st[0, f, pl.ds((G - d) * K, K), :] = recv_s[src, :]

    def unpack_corner(src, row_of):
        edge = pltpu.roll(src[pl.ds(24, 8), :], 124, 1)
        for d in range(1, G + 1):
            bq[pl.ds(row_of(d), 1), :] = edge[d - 1 : d]
        for d in range(1, G):
            both = src[pl.ds(8 * (d - 1), 8), :]
            for g in range(16):
                f, kb = g // 4, KB[g % 4]
                q_st[0, f, pl.ds(row_of(d) * K + kb, 8), :] = pltpu.roll(both, (124 - 8 * g) % 128, 1)

    def north_row(d):
        return G + R - 1 + d

    def south_row(d):
        return G - d

    wait_rows(0)
    wait_rows(4)
    for d in range(1, G + 1):
        bm[pl.ds(north_row(d), 1), :] = recv_n[pl.ds(d - 1, 1), :]
    unpack_corner(crecv_n, north_row)

    @pl.when(has_south)
    def _():
        for d in range(1, G + 1):
            bm[pl.ds(south_row(d), 1), :] = recv_s[pl.ds(d - 1, 1), :]
        unpack_corner(crecv_s, south_row)

    sides_of_bottom((0, 16))
    mask_loop(1, G + 1)
    mask_loop(G + R - 1, 2 * G + R - 1)
    for d in range(1, G):
        if d > 1:
            wait_rows(d - 1)
        unpack_rows(d)
    for s in range(SWEEPS):
        for row in (south_row(G - 1 - s), north_row(1 - s)):
            pressure(s, row * K, 3, K)
        for row in (south_row(2 - s), north_row(-s)):
            for b in (row * K, row * K + 35):
                update(s, b, 40, s < SWEEPS - 1, 40)

    wait_rows(G - 1)
    unpack_rows(G)
    for s in range(SWEEPS):
        d = G - s
        pressure(s, south_row(d) * K, 2, (north_row(d) - south_row(d)) * K)
        for row in (south_row(d - 1), north_row(d - 1)):
            update(s, row * K, 32, False, K)

    to_east.wait_send()
    to_west.wait_send()
    for q in range(G):

        @pl.when(relays)
        def _():
            passed(q).wait_send()

    for q in range(G + 1):
        wait_sent(q)


def write_out(m4, t_out, s_out, u_out, v_out):
    for f, out in enumerate((t_out, s_out, u_out, v_out)):
        for k in range(K):
            for h in range(2):
                out[k, pl.ds(8 * h, 8), :] = m4[f, pl.ds(8 * h * K + k, 8, stride=K), :]


def per_device(n_lon, n_lat, t, s, u, v, water_indicator, bottom):
    del water_indicator
    f32 = jnp.float32
    hbm = pl.BlockSpec(memory_space=pl.ANY)
    vmem = pltpu.VMEM
    dma = pltpu.SemaphoreType.DMA
    states = pl.pallas_call(
        functools.partial(kernel, n_lon, n_lat),
        out_shape=pltpu.VMEM((4, R * K, 128), f32),
        in_specs=[hbm] * 5,
        out_specs=pl.BlockSpec(memory_space=pltpu.VMEM),
        scratch_shapes=[
            vmem((4, K, R, 128), f32), vmem((R, 128), jnp.int32),
            vmem((SWEEPS, 4, LIN, 128), f32), vmem((SWEEPS, 4, LIN, 128), f32),
            vmem((SWEEPS, LIN, 128), f32), vmem((SWEEPS, LIN, 128), f32),
            vmem((N_MASK, LIN, 128), f32), vmem((N_MASK, LIN, 128), f32), vmem((LIN, 128), f32),
            vmem((32, 128), f32), vmem((32, 128), f32), vmem((4, 32, 128), f32),
            vmem((PACKED, 128), f32), vmem((PACKED, 128), f32), vmem((PACKED, 128), f32),
            *[vmem((MSG, 128), f32)] * 5,
            vmem((CORNER, 128), f32), vmem((CORNER, 128), f32), vmem((CORNER, 128), f32), vmem((CORNER, 128), f32),
            dma((5,)), dma((2,)), dma((2,)), dma((5,)), dma((5,)), dma((5,)), dma((5,)), dma((G,)), dma((G,)),
        ],
        compiler_params=pltpu.CompilerParams(
            collective_id=1, has_side_effects=True, vmem_limit_bytes=48 * 1024 * 1024
        ),
        name="sweeps",
    )(*(pltpu.with_memory_space_constraint(x, pltpu.HBM) for x in (t, s, u, v, bottom)))
    field = jax.ShapeDtypeStruct((K, R, 128), f32)
    return tuple(
        pl.pallas_call(
            write_out,
            out_shape=[field] * 4,
            compiler_params=pltpu.CompilerParams(vmem_limit_bytes=16 * 1024 * 1024),
            name="write_out",
        )(states)
    )


def solution(mesh):
    field = P(None, LAT, LON)
    return jax.shard_map(
        functools.partial(per_device, mesh.shape[LON], mesh.shape[LAT]),
        mesh=mesh,
        in_specs=(field,) * 5 + (P(LAT, LON),),
        out_specs=(field,) * 4,
        check_vma=False,
    )
```

```python
import functools

import jax
import jax.numpy as jnp
from jax import lax
from jax.experimental import pallas as pl
from jax.experimental.pallas import tpu as pltpu
from jax.sharding import PartitionSpec as P

SWEEPS = 4

courant = 0.3
mixing = 0.08
vertical_mixing = 0.1
buoyancy = 0.05
rotation = 0.2
drag_rate = 0.3
thermal = 0.25
haline = 0.2
cabbeling = 0.03

K = 25
R = 16
G = 4
LIN = (R + 2 * G) * K + 16
BLOCK = 56
HEAD = 8
CHUNKS = ((0, 112), (112, 96), (208, 104), (312, 96))
MSG = 408
PACKED = 104
CORNER = 32
KB = (0, 8, 16, 17)
N_MASK = 8

LON, LAT = "lon", "lat"


def lane(shape):
    return lax.broadcasted_iota(jnp.int32, shape, 1)


def density(t, s):
    h = 0.5 * buoyancy
    return t * (-thermal * h - (cabbeling * h) * t) + (haline * h) * s


def kernel(
    n_lon, n_lat, t_hbm, s_hbm, u_hbm, v_hbm, b_hbm, m4,
    xin, bin_, m_st, q_st, pm, pq, mk, qk, cor, bm, bq, b_side,
    pack, pack_w, pack_e, send_n, send_s, recv_n, recv_s, passing, csend_n, csend_s, crecv_n, crecv_s,
    in_sem, lon_ss, lon_rs, n_ss, n_rs, s_ss, s_rs, pass_ss, pass_rs,
):
    i = lax.axis_index(LON)
    j = lax.axis_index(LAT)
    top = j == n_lat - 1
    east = lax.rem(i + 1, n_lon)
    west = lax.rem(i + n_lon - 1, n_lon)
    has_south = j > 0
    north = {LON: jnp.where(top, n_lon - 1 - i, i), LAT: jnp.where(top, j, j + 1)}
    south = {LON: i, LAT: jnp.maximum(j - 1, 0)}
    mesh_id = pl.DeviceIdType.MESH
    across = {LON: lax.rem(i + n_lon // 2, n_lon), LAT: j}
    relay = {LON: n_lon - 1 - lax.rem(i + n_lon // 2, n_lon), LAT: j}

    barrier = pltpu.get_barrier_semaphore()
    pl.semaphore_signal(barrier, inc=1, device_id={LON: east, LAT: j}, device_id_type=mesh_id)
    pl.semaphore_signal(barrier, inc=1, device_id={LON: west, LAT: j}, device_id_type=mesh_id)
    pl.semaphore_signal(barrier, inc=1, device_id=north, device_id_type=mesh_id)

    @pl.when(has_south)
    def _():
        pl.semaphore_signal(barrier, inc=1, device_id=south, device_id_type=mesh_id)

    @pl.when(top)
    def _():
        pl.semaphore_signal(barrier, inc=1, device_id=across, device_id_type=mesh_id)
        pl.semaphore_signal(barrier, inc=1, device_id=relay, device_id_type=mesh_id)

    loads = [
        pltpu.make_async_copy(ref, xin.at[f], in_sem.at[f])
        for f, ref in enumerate((t_hbm, s_hbm, u_hbm, v_hbm))
    ]
    loads.append(pltpu.make_async_copy(b_hbm, bin_, in_sem.at[4]))
    for c in loads:
        c.start()
    for c in loads:
        c.wait()

    lanes8 = lane((8, 128))
    group8 = lanes8 // 8

    bm[pl.ds(G, R), :] = bin_[...].astype(jnp.float32)
    tiles = [(f, k, h) for f in range(4) for k in range(K) for h in range(2)]
    tiles += [(4, 0, 0), (4, 0, 1)]
    acc = None
    for n, (f, k, h) in enumerate(tiles):
        if f < 4:
            v = xin[f, k, pl.ds(8 * h, 8), :]
            m_st[0, f, pl.ds((G + 8 * h) * K + k, 8, stride=K), :] = v
        else:
            v = bm[pl.ds(G + 8 * h, 8), :]
        g = n % 16
        rolled = pltpu.roll(v, 4 + 8 * g, 1)
        acc = rolled if g == 0 else jnp.where(group8 == g, rolled, acc)
        if g == 15 or n == len(tiles) - 1:
            pack[pl.ds(8 * (n // 16), 8), :] = acc

    sign = jnp.where(top, -1.0, 1.0).astype(jnp.float32)
    lanes32 = lane((32, 128))
    turn32 = jnp.where(top, 127 - lanes32, lanes32)
    turn8 = jnp.where(top, 127 - lanes8, lanes8)
    sub8 = lax.broadcasted_iota(jnp.int32, (8, 128), 0)

    def turned(v, idx):
        return jnp.take_along_axis(v, idx, axis=1, mode="promise_in_bounds")

    edge = jnp.zeros((8, 128), jnp.float32)
    for d in range(1, G + 1):
        edge = jnp.where(sub8 == d - 1, bm[pl.ds(G + R - d, 1), :], edge)
    send_n[pl.ds(0, 8), :] = turned(edge, turn8)
    send_s[pl.ds(0, 8), :] = bm[pl.ds(G, 8), :]
    for d in range(1, G + 1):
        for f in range(4):
            at = HEAD + (d - 1) * 100 + f * K
            v = turned(m_st[0, f, pl.ds((G + R - d) * K, 32), :], turn32)
            if f >= 2:
                v = v * sign
            send_n[pl.ds(at, K), :] = v[:K]
            send_s[pl.ds(at, K), :] = m_st[0, f, pl.ds((G + d - 1) * K, K), :]

    pl.semaphore_wait(barrier, jnp.where(has_south, 4, 3) + jnp.where(top, 2, 0))

    def remote(src, dst, ss, rs, to):
        return pltpu.make_async_remote_copy(
            src_ref=src, dst_ref=dst, send_sem=ss, recv_sem=rs, device_id=to, device_id_type=mesh_id
        )

    to_east = remote(pack, pack_w, lon_ss.at[0], lon_rs.at[0], {LON: east, LAT: j})
    to_west = remote(pack, pack_e, lon_ss.at[1], lon_rs.at[1], {LON: west, LAT: j})
    to_east.start()
    to_west.start()

    def row_pieces(q):
        if q < G:
            sl = pl.ds(*CHUNKS[q])
            return send_n.at[sl], send_s.at[sl], recv_n.at[sl], recv_s.at[sl]
        return csend_n, csend_s, crecv_n, crecv_s

    def start_north(q):
        sn, ss, rn, rs = row_pieces(q)

        @pl.when(jnp.logical_not(top))
        def _():
            remote(sn, rs, n_ss.at[q], s_rs.at[q], north).start()

        @pl.when(top)
        def _():
            if q == G:
                remote(sn, rn, n_ss.at[q], n_rs.at[q], north).start()
            else:
                remote(sn, passing.at[pl.ds(*CHUNKS[q])], n_ss.at[q], pass_rs.at[q], relay).start()

    def start_south(q):
        sn, ss, rn, rs = row_pieces(q)

        @pl.when(has_south)
        def _():
            remote(ss, rn, s_ss.at[q], n_rs.at[q], south).start()

    def start_rows(q):
        start_north(q)
        start_south(q)

    def wait_rows(q):
        sn, ss, rn, rs = row_pieces(q)
        remote(ss, rn, s_ss.at[q], n_rs.at[q], north).wait_recv()

        @pl.when(has_south)
        def _():
            remote(sn, rs, n_ss.at[q], s_rs.at[q], south).wait_recv()

    def passed(q):
        sl = pl.ds(*CHUNKS[q])
        return remote(passing.at[sl], recv_n.at[sl], pass_ss.at[q], n_rs.at[q], across)

    def pass_on(q):
        @pl.when(top)
        def _():
            sl = pl.ds(*CHUNKS[q])
            remote(send_n.at[sl], passing.at[sl], n_ss.at[q], pass_rs.at[q], relay).wait_recv()
            passed(q).start()

    def wait_sent(q):
        sn, ss, rn, rs = row_pieces(q)
        remote(sn, rs, n_ss.at[q], s_rs.at[q], north).wait_send()

        @pl.when(has_south)
        def _():
            remote(ss, rn, s_ss.at[q], n_rs.at[q], south).wait_send()

    start_rows(0)
    start_rows(1)

    @pl.when(jnp.logical_not(has_south))
    def _():
        zero = jnp.zeros((G * K, 128), jnp.float32)
        bm[pl.ds(0, G), :] = zero[:G]
        bq[pl.ds(0, G), :] = zero[:G]
        for f in range(4):
            m_st[0, f, pl.ds(0, G * K), :] = zero
            q_st[0, f, pl.ds(0, G * K), :] = zero

    to_east.wait_recv()
    to_west.wait_recv()
    west_half = lanes8 % 8 < 4
    for q in range(PACKED // 8):
        both = jnp.where(west_half, pack_w[pl.ds(8 * q, 8), :], pack_e[pl.ds(8 * q, 8), :])
        for g in range(16):
            n = 16 * q + g
            if n >= len(tiles):
                break
            f, k, h = tiles[n]
            v = pltpu.roll(both, (124 - 8 * g) % 128, 1)
            if f < 4:
                q_st[0, f, pl.ds((G + 8 * h) * K + k, 8, stride=K), :] = v
            else:
                bq[pl.ds(G + 8 * h, 8), :] = v

    flip8 = jnp.where(top, lanes8 + 7 - 2 * (lanes8 % 8), lanes8)
    sign8 = jnp.where(lanes8 >= 64, sign, 1.0)
    for d in range(1, G):
        acc_n = acc_s = None
        for g in range(16):
            f, kb = g // 4, KB[g % 4]
            vn = pltpu.roll(q_st[0, f, pl.ds((G + R - d) * K + kb, 8), :], 4 + 8 * g, 1)
            vs = pltpu.roll(q_st[0, f, pl.ds((G + d - 1) * K + kb, 8), :], 4 + 8 * g, 1)
            acc_n = vn if g == 0 else jnp.where(group8 == g, vn, acc_n)
            acc_s = vs if g == 0 else jnp.where(group8 == g, vs, acc_s)
        csend_n[pl.ds(8 * (d - 1), 8), :] = turned(acc_n, flip8) * sign8
        csend_s[pl.ds(8 * (d - 1), 8), :] = acc_s
    edge = jnp.zeros((8, 128), jnp.float32)
    for d in range(1, G + 1):
        edge = jnp.where(sub8 == d - 1, bq[pl.ds(G + R - d, 1), :], edge)
    csend_n[pl.ds(24, 8), :] = turned(pltpu.roll(edge, 4, 1), flip8)
    csend_s[pl.ds(24, 8), :] = pltpu.roll(bq[pl.ds(G, 8), :], 4, 1)
    start_rows(4)
    start_north(2)
    start_north(3)
    pass_on(0)
    pass_on(1)
    start_south(2)
    start_south(3)

    kk = lax.broadcasted_iota(jnp.int32, (32, 128), 0).astype(jnp.float32)
    firstb = lane((BLOCK, 128)) == 0
    lastb = lane((BLOCK, 128)) == 127
    total_rows = n_lat * R

    def sides_of_bottom(rows):
        for r in rows:
            sl = pl.ds(r, 8)
            m, q = bm[sl, :], bq[sl, :]
            first, last = lanes8 == 0, lanes8 == 127
            b_side[0, sl, :] = pltpu.roll(jnp.where(first, q, m), 127, 1)
            b_side[1, sl, :] = pltpu.roll(jnp.where(last, q, m), 1, 1)
            b_side[2, sl, :] = pltpu.roll(jnp.where(first, m, q), 127, 1)
            b_side[3, sl, :] = pltpu.roll(jnp.where(last, m, q), 1, 1)

    def masks(r):
        at = r * K
        one = pl.ds(r, 1)
        sides = (
            (mk, bm[one, :], b_side[0, one, :], b_side[1, one, :], bm),
            (qk, bq[one, :], b_side[2, one, :], b_side[3, one, :], bq),
        )
        for store, c, e, w, rows in sides:
            n, s = rows[pl.ds(r + 1, 1), :], rows[pl.ds(r - 1, 1), :]

            def flag(x):
                return jnp.where(kk < x, 1.0, 0.0)

            wet = flag(c)
            vu = jnp.where(kk >= 1.0, vertical_mixing * wet, 0.0)
            vd = vertical_mixing * flag(c - 1.0)
            drag = jnp.where(kk == c - 1.0, 1.0 - drag_rate, 1.0)
            for q, x in enumerate(
                (
                    flag(jnp.minimum(c, e)), flag(jnp.minimum(c, w)), flag(jnp.minimum(c, n)), flag(jnp.minimum(c, s)),
                    vu, vd, wet - vu - vd, wet * drag,
                )
            ):
                store[q, pl.ds(at, K), :] = x[:K]
        row = j * R + r - G
        row = jnp.where(row >= total_rows, 2 * total_rows - 1 - row, row)
        f = rotation * (2.0 * (row.astype(jnp.float32) + 0.5) / total_rows - 1.0)
        cor[pl.ds(at, K), :] = jnp.full((K, 128), 1.0, jnp.float32) * f

    def pressure(s, start, count, stride):
        for st, out in ((m_st, pm), (q_st, pq)):
            total = None
            for k in range(K):
                sl = pl.ds(start + k, count, stride=stride)
                x = density(st[s, 0, sl, :], st[s, 1, sl, :])
                total = x if total is None else total + x
                out[s, sl, :] = total

    def update(s, b, size, with_q, keep):
        first, last = firstb[:size], lastb[:size]
        sl = pl.ds(b, size)
        mc = [m_st[s, f, sl, :] for f in range(4)] + [pm[s, sl, :]]
        qc = [q_st[s, f, sl, :] for f in range(4)] + [pq[s, sl, :]]
        m_e, m_w, q_e, q_w = [], [], [], []
        for m, q in zip(mc, qc):
            me, mw = pltpu.roll(m, 127, 1), pltpu.roll(m, 1, 1)
            qe, qw = pltpu.roll(q, 127, 1), pltpu.roll(q, 1, 1)
            m_e.append(jnp.where(last, qe, me))
            m_w.append(jnp.where(first, qw, mw))
            if with_q:
                q_e.append(jnp.where(last, me, qe))
                q_w.append(jnp.where(first, mw, qw))
        work = [(m_st, pm, mk, mc, m_e, m_w)]
        if with_q:
            work.append((q_st, pq, qk, qc, q_e, q_w))
        for st, pr, mask, c, e, w in work:
            fe, fw, fn, fs, vu, vd, w0, wd = [mask[q, sl, :] for q in range(N_MASK)]
            a, b_ = courant * c[2], courant * c[3]
            a_neg, b_neg = jnp.minimum(a, 0.0), jnp.minimum(b_, 0.0)
            ce = fe * (mixing - a_neg)
            cw = fw * (mixing + (a - a_neg))
            cn = fn * (mixing - b_neg)
            cs = fs * (mixing + (b_ - b_neg))
            c0 = w0 - ((ce + cw) + (cn + cs))
            north_sl, south_sl = pl.ds(b + K, size), pl.ds(b - K, size)
            new = []
            for f in range(4):
                x = (c0 * c[f] + ce * e[f]) + (cw * w[f] + cn * st[s, f, north_sl, :])
                x = x + (cs * st[s, f, south_sl, :] + vu * st[s, f, pl.ds(b - 1, size), :])
                new.append(x + vd * st[s, f, pl.ds(b + 1, size), :])
            p = c[4]
            px = fe * (e[4] - p) + fw * (p - w[4])
            py = fn * (pr[s, north_sl, :] - p) + fs * (p - pr[s, south_sl, :])
            f0 = cor[sl, :]
            new[2] = wd * (new[2] + f0 * c[3] - px)
            new[3] = wd * (new[3] - f0 * c[2] - py)
            for f in range(4):
                if s < SWEEPS - 1:
                    st[s + 1, f, pl.ds(b, keep), :] = new[f][:keep]
                else:
                    m4[f, pl.ds(b - G * K, keep), :] = new[f][:keep]

    def mask_loop(lo, hi):
        def body(r, carry):
            masks(r)
            return carry

        lax.fori_loop(lo, hi, body, 0)

    sides_of_bottom((G, G + 8))
    mask_loop(G + 1, G + R - 1)
    for s in range(SWEEPS):
        count = R - 2 * s
        pressure(s, (G + s) * K, 8, K)
        pressure(s, (G + R - s - 8) * K, 8, K)
        lo, hi = (G + s + 1) * K, (G + R - s - 1) * K
        steps = -(-(hi - lo) // BLOCK)

        def body(t, carry, s=s, lo=lo, hi=hi):
            b = jnp.minimum(lo + t * BLOCK, hi - BLOCK)
            update(s, b, BLOCK, s < SWEEPS - 1, BLOCK)
            return carry

        lax.fori_loop(0, steps, body, 0)
        if s in (0, 1):
            pass_on(s + 2)

    def unpack_rows(d):
        for f in range(4):
            src = pl.ds(HEAD + (d - 1) * 100 + f * K, K)
            m_st[0, f, pl.ds((G + R - 1 + d) * K, K), :] = recv_n[src, :]

        @pl.when(has_south)
        def _():
            for f in range(4):
                src = pl.ds(HEAD + (d - 1) * 100 + f * K, K)
                m_st[0, f, pl.ds((G - d) * K, K), :] = recv_s[src, :]

    def unpack_corner(src, row_of):
        edge = pltpu.roll(src[pl.ds(24, 8), :], 124, 1)
        for d in range(1, G + 1):
            bq[pl.ds(row_of(d), 1), :] = edge[d - 1 : d]
        for d in range(1, G):
            both = src[pl.ds(8 * (d - 1), 8), :]
            for g in range(16):
                f, kb = g // 4, KB[g % 4]
                q_st[0, f, pl.ds(row_of(d) * K + kb, 8), :] = pltpu.roll(both, (124 - 8 * g) % 128, 1)

    def north_row(d):
        return G + R - 1 + d

    def south_row(d):
        return G - d

    wait_rows(0)
    wait_rows(4)
    for d in range(1, G + 1):
        bm[pl.ds(north_row(d), 1), :] = recv_n[pl.ds(d - 1, 1), :]
    unpack_corner(crecv_n, north_row)

    @pl.when(has_south)
    def _():
        for d in range(1, G + 1):
            bm[pl.ds(south_row(d), 1), :] = recv_s[pl.ds(d - 1, 1), :]
        unpack_corner(crecv_s, south_row)

    sides_of_bottom((0, 16))
    mask_loop(1, G + 1)
    mask_loop(G + R - 1, 2 * G + R - 1)
    for d in range(1, G):
        if d > 1:
            wait_rows(d - 1)
        unpack_rows(d)
    for s in range(SWEEPS):
        for row in (south_row(G - 1 - s), north_row(1 - s)):
            pressure(s, row * K, 3, K)
        for row in (south_row(2 - s), north_row(-s)):
            for b in (row * K, row * K + 35):
                update(s, b, 40, s < SWEEPS - 1, 40)

    wait_rows(G - 1)
    unpack_rows(G)
    for s in range(SWEEPS):
        d = G - s
        pressure(s, south_row(d) * K, 2, (north_row(d) - south_row(d)) * K)
        for row in (south_row(d - 1), north_row(d - 1)):
            update(s, row * K, 32, False, K)

    to_east.wait_send()
    to_west.wait_send()
    for q in range(G):

        @pl.when(top)
        def _():
            passed(q).wait_send()

    for q in range(G + 1):
        wait_sent(q)


def write_out(m4, t_out, s_out, u_out, v_out):
    for f, out in enumerate((t_out, s_out, u_out, v_out)):
        for k in range(K):
            for h in range(2):
                out[k, pl.ds(8 * h, 8), :] = m4[f, pl.ds(8 * h * K + k, 8, stride=K), :]


def per_device(n_lon, n_lat, t, s, u, v, water_indicator, bottom):
    del water_indicator
    f32 = jnp.float32
    hbm = pl.BlockSpec(memory_space=pl.ANY)
    vmem = pltpu.VMEM
    dma = pltpu.SemaphoreType.DMA
    states = pl.pallas_call(
        functools.partial(kernel, n_lon, n_lat),
        out_shape=pltpu.VMEM((4, R * K, 128), f32),
        in_specs=[hbm] * 5,
        out_specs=pl.BlockSpec(memory_space=pltpu.VMEM),
        scratch_shapes=[
            vmem((4, K, R, 128), f32), vmem((R, 128), jnp.int32),
            vmem((SWEEPS, 4, LIN, 128), f32), vmem((SWEEPS, 4, LIN, 128), f32),
            vmem((SWEEPS, LIN, 128), f32), vmem((SWEEPS, LIN, 128), f32),
            vmem((N_MASK, LIN, 128), f32), vmem((N_MASK, LIN, 128), f32), vmem((LIN, 128), f32),
            vmem((32, 128), f32), vmem((32, 128), f32), vmem((4, 32, 128), f32),
            vmem((PACKED, 128), f32), vmem((PACKED, 128), f32), vmem((PACKED, 128), f32),
            *[vmem((MSG, 128), f32)] * 5,
            vmem((CORNER, 128), f32), vmem((CORNER, 128), f32), vmem((CORNER, 128), f32), vmem((CORNER, 128), f32),
            dma((5,)), dma((2,)), dma((2,)), dma((5,)), dma((5,)), dma((5,)), dma((5,)), dma((G,)), dma((G,)),
        ],
        compiler_params=pltpu.CompilerParams(
            collective_id=1, has_side_effects=True, vmem_limit_bytes=48 * 1024 * 1024
        ),
        name="sweeps",
    )(*(pltpu.with_memory_space_constraint(x, pltpu.HBM) for x in (t, s, u, v, bottom)))
    field = jax.ShapeDtypeStruct((K, R, 128), f32)
    return tuple(
        pl.pallas_call(
            write_out,
            out_shape=[field] * 4,
            compiler_params=pltpu.CompilerParams(vmem_limit_bytes=16 * 1024 * 1024),
            name="write_out",
        )(states)
    )


def solution(mesh):
    field = P(None, LAT, LON)
    return jax.shard_map(
        functools.partial(per_device, mesh.shape[LON], mesh.shape[LAT]),
        mesh=mesh,
        in_specs=(field,) * 5 + (P(LAT, LON),),
        out_specs=(field,) * 4,
        check_vma=False,
    )
```

```python
import functools

import jax
import jax.numpy as jnp
from jax import lax
from jax.experimental import pallas as pl
from jax.experimental.pallas import tpu as pltpu
from jax.sharding import PartitionSpec as P

SWEEPS = 4

courant = 0.3
mixing = 0.08
vertical_mixing = 0.1
buoyancy = 0.05
rotation = 0.2
drag_rate = 0.3
thermal = 0.25
haline = 0.2
cabbeling = 0.03

K = 25
R = 16
G = 4
LIN = (R + 2 * G) * K + 16
BLOCK = 56
HEAD = 8
CHUNKS = ((0, 112), (112, 96), (208, 104), (312, 96))
MSG = 408
PACKED = 104
CORNER = 32
KB = (0, 8, 16, 17)
N_MASK = 8

LON, LAT = "lon", "lat"


def lane(shape):
    return lax.broadcasted_iota(jnp.int32, shape, 1)


def density(t, s):
    h = 0.5 * buoyancy
    return t * (-thermal * h - (cabbeling * h) * t) + (haline * h) * s


def kernel(
    n_lon, n_lat, t_hbm, s_hbm, u_hbm, v_hbm, b_hbm, m4,
    xin, bin_, m_st, q_st, pm, pq, mk, qk, cor, bm, bq, b_side,
    pack, pack_w, pack_e, send_n, send_s, recv_n, recv_s, passing, csend_n, csend_s, crecv_n, crecv_s,
    in_sem, lon_ss, lon_rs, n_ss, n_rs, s_ss, s_rs, pass_ss, pass_rs,
):
    i = lax.axis_index(LON)
    j = lax.axis_index(LAT)
    top = j == n_lat - 1
    east = lax.rem(i + 1, n_lon)
    west = lax.rem(i + n_lon - 1, n_lon)
    has_south = j > 0
    north = {LON: jnp.where(top, n_lon - 1 - i, i), LAT: jnp.where(top, j, j + 1)}
    south = {LON: i, LAT: jnp.maximum(j - 1, 0)}
    mesh_id = pl.DeviceIdType.MESH
    passes = j == 1
    half_on = lax.rem(i + n_lon // 2, n_lon)
    mirrored = n_lon - 1 - i
    fold_to = {LON: half_on, LAT: jnp.int32(1)}
    fold_from = {LON: lax.rem(mirrored + n_lon // 2, n_lon), LAT: jnp.int32(1)}
    pass_from = {LON: half_on, LAT: jnp.int32(n_lat - 1)}
    pass_to = {LON: n_lon - 1 - half_on, LAT: jnp.int32(n_lat - 1)}

    barrier = pltpu.get_barrier_semaphore()
    pl.semaphore_signal(barrier, inc=1, device_id={LON: east, LAT: j}, device_id_type=mesh_id)
    pl.semaphore_signal(barrier, inc=1, device_id={LON: west, LAT: j}, device_id_type=mesh_id)
    pl.semaphore_signal(barrier, inc=1, device_id=north, device_id_type=mesh_id)

    @pl.when(has_south)
    def _():
        pl.semaphore_signal(barrier, inc=1, device_id=south, device_id_type=mesh_id)

    for here, first, second in ((top, fold_to, fold_from), (passes, pass_from, pass_to)):

        @pl.when(here)
        def _(first=first, second=second):
            pl.semaphore_signal(barrier, inc=1, device_id=first, device_id_type=mesh_id)
            pl.semaphore_signal(barrier, inc=1, device_id=second, device_id_type=mesh_id)

    loads = [
        pltpu.make_async_copy(ref, xin.at[f], in_sem.at[f])
        for f, ref in enumerate((t_hbm, s_hbm, u_hbm, v_hbm))
    ]
    loads.append(pltpu.make_async_copy(b_hbm, bin_, in_sem.at[4]))
    for c in loads:
        c.start()
    for c in loads:
        c.wait()

    lanes8 = lane((8, 128))
    group8 = lanes8 // 8

    bm[pl.ds(G, R), :] = bin_[...].astype(jnp.float32)
    tiles = [(f, k, h) for f in range(4) for k in range(K) for h in range(2)]
    tiles += [(4, 0, 0), (4, 0, 1)]
    acc = None
    for n, (f, k, h) in enumerate(tiles):
        if f < 4:
            v = xin[f, k, pl.ds(8 * h, 8), :]
            m_st[0, f, pl.ds((G + 8 * h) * K + k, 8, stride=K), :] = v
        else:
            v = bm[pl.ds(G + 8 * h, 8), :]
        g = n % 16
        rolled = pltpu.roll(v, 4 + 8 * g, 1)
        acc = rolled if g == 0 else jnp.where(group8 == g, rolled, acc)
        if g == 15 or n == len(tiles) - 1:
            pack[pl.ds(8 * (n // 16), 8), :] = acc

    sign = jnp.where(top, -1.0, 1.0).astype(jnp.float32)
    lanes32 = lane((32, 128))
    turn32 = jnp.where(top, 127 - lanes32, lanes32)
    turn8 = jnp.where(top, 127 - lanes8, lanes8)
    sub8 = lax.broadcasted_iota(jnp.int32, (8, 128), 0)

    def turned(v, idx):
        return jnp.take_along_axis(v, idx, axis=1, mode="promise_in_bounds")

    edge = jnp.zeros((8, 128), jnp.float32)
    for d in range(1, G + 1):
        edge = jnp.where(sub8 == d - 1, bm[pl.ds(G + R - d, 1), :], edge)
    send_n[pl.ds(0, 8), :] = turned(edge, turn8)
    send_s[pl.ds(0, 8), :] = bm[pl.ds(G, 8), :]
    for d in range(1, G + 1):
        for f in range(4):
            at = HEAD + (d - 1) * 100 + f * K
            v = turned(m_st[0, f, pl.ds((G + R - d) * K, 32), :], turn32)
            if f >= 2:
                v = v * sign
            send_n[pl.ds(at, K), :] = v[:K]
            send_s[pl.ds(at, K), :] = m_st[0, f, pl.ds((G + d - 1) * K, K), :]

    pl.semaphore_wait(barrier, jnp.where(has_south, 4, 3) + jnp.where(jnp.logical_or(top, passes), 2, 0))

    def remote(src, dst, ss, rs, to):
        return pltpu.make_async_remote_copy(
            src_ref=src, dst_ref=dst, send_sem=ss, recv_sem=rs, device_id=to, device_id_type=mesh_id
        )

    to_east = remote(pack, pack_w, lon_ss.at[0], lon_rs.at[0], {LON: east, LAT: j})
    to_west = remote(pack, pack_e, lon_ss.at[1], lon_rs.at[1], {LON: west, LAT: j})
    to_east.start()
    to_west.start()

    def row_pieces(q):
        if q < G:
            sl = pl.ds(*CHUNKS[q])
            return send_n.at[sl], send_s.at[sl], recv_n.at[sl], recv_s.at[sl]
        return csend_n, csend_s, crecv_n, crecv_s

    def start_north(q):
        sn, ss, rn, rs = row_pieces(q)

        @pl.when(jnp.logical_not(top))
        def _():
            remote(sn, rs, n_ss.at[q], s_rs.at[q], north).start()

        @pl.when(top)
        def _():
            if q == G:
                remote(sn, rn, n_ss.at[q], n_rs.at[q], north).start()
            else:
                remote(sn, passing.at[pl.ds(*CHUNKS[q])], n_ss.at[q], pass_rs.at[q], fold_to).start()

    def start_south(q):
        sn, ss, rn, rs = row_pieces(q)

        @pl.when(has_south)
        def _():
            remote(ss, rn, s_ss.at[q], n_rs.at[q], south).start()

    def start_rows(q):
        start_north(q)
        start_south(q)

    def wait_rows(q):
        sn, ss, rn, rs = row_pieces(q)
        remote(ss, rn, s_ss.at[q], n_rs.at[q], north).wait_recv()

        @pl.when(has_south)
        def _():
            remote(sn, rs, n_ss.at[q], s_rs.at[q], south).wait_recv()

    def passed(q):
        sl = pl.ds(*CHUNKS[q])
        return remote(passing.at[sl], recv_n.at[sl], pass_ss.at[q], n_rs.at[q], pass_to)

    def pass_on(q):
        @pl.when(passes)
        def _():
            sl = pl.ds(*CHUNKS[q])
            remote(send_n.at[sl], passing.at[sl], n_ss.at[q], pass_rs.at[q], pass_from).wait_recv()
            passed(q).start()

    def wait_sent(q):
        sn, ss, rn, rs = row_pieces(q)
        remote(sn, rs, n_ss.at[q], s_rs.at[q], north).wait_send()

        @pl.when(has_south)
        def _():
            remote(ss, rn, s_ss.at[q], n_rs.at[q], south).wait_send()

    start_rows(0)
    start_rows(1)

    @pl.when(jnp.logical_not(has_south))
    def _():
        zero = jnp.zeros((G * K, 128), jnp.float32)
        bm[pl.ds(0, G), :] = zero[:G]
        bq[pl.ds(0, G), :] = zero[:G]
        for f in range(4):
            m_st[0, f, pl.ds(0, G * K), :] = zero
            q_st[0, f, pl.ds(0, G * K), :] = zero

    to_east.wait_recv()
    to_west.wait_recv()
    west_half = lanes8 % 8 < 4
    for q in range(PACKED // 8):
        both = jnp.where(west_half, pack_w[pl.ds(8 * q, 8), :], pack_e[pl.ds(8 * q, 8), :])
        for g in range(16):
            n = 16 * q + g
            if n >= len(tiles):
                break
            f, k, h = tiles[n]
            v = pltpu.roll(both, (124 - 8 * g) % 128, 1)
            if f < 4:
                q_st[0, f, pl.ds((G + 8 * h) * K + k, 8, stride=K), :] = v
            else:
                bq[pl.ds(G + 8 * h, 8), :] = v

    flip8 = jnp.where(top, lanes8 + 7 - 2 * (lanes8 % 8), lanes8)
    sign8 = jnp.where(lanes8 >= 64, sign, 1.0)
    for d in range(1, G):
        acc_n = acc_s = None
        for g in range(16):
            f, kb = g // 4, KB[g % 4]
            vn = pltpu.roll(q_st[0, f, pl.ds((G + R - d) * K + kb, 8), :], 4 + 8 * g, 1)
            vs = pltpu.roll(q_st[0, f, pl.ds((G + d - 1) * K + kb, 8), :], 4 + 8 * g, 1)
            acc_n = vn if g == 0 else jnp.where(group8 == g, vn, acc_n)
            acc_s = vs if g == 0 else jnp.where(group8 == g, vs, acc_s)
        csend_n[pl.ds(8 * (d - 1), 8), :] = turned(acc_n, flip8) * sign8
        csend_s[pl.ds(8 * (d - 1), 8), :] = acc_s
    edge = jnp.zeros((8, 128), jnp.float32)
    for d in range(1, G + 1):
        edge = jnp.where(sub8 == d - 1, bq[pl.ds(G + R - d, 1), :], edge)
    csend_n[pl.ds(24, 8), :] = turned(pltpu.roll(edge, 4, 1), flip8)
    csend_s[pl.ds(24, 8), :] = pltpu.roll(bq[pl.ds(G, 8), :], 4, 1)
    start_rows(4)
    start_north(2)
    start_north(3)
    pass_on(0)
    pass_on(1)
    start_south(2)
    start_south(3)

    kk = lax.broadcasted_iota(jnp.int32, (32, 128), 0).astype(jnp.float32)
    firstb = lane((BLOCK, 128)) == 0
    lastb = lane((BLOCK, 128)) == 127
    total_rows = n_lat * R

    def sides_of_bottom(rows):
        for r in rows:
            sl = pl.ds(r, 8)
            m, q = bm[sl, :], bq[sl, :]
            first, last = lanes8 == 0, lanes8 == 127
            b_side[0, sl, :] = pltpu.roll(jnp.where(first, q, m), 127, 1)
            b_side[1, sl, :] = pltpu.roll(jnp.where(last, q, m), 1, 1)
            b_side[2, sl, :] = pltpu.roll(jnp.where(first, m, q), 127, 1)
            b_side[3, sl, :] = pltpu.roll(jnp.where(last, m, q), 1, 1)

    def masks(r):
        at = r * K
        one = pl.ds(r, 1)
        sides = (
            (mk, bm[one, :], b_side[0, one, :], b_side[1, one, :], bm),
            (qk, bq[one, :], b_side[2, one, :], b_side[3, one, :], bq),
        )
        for store, c, e, w, rows in sides:
            n, s = rows[pl.ds(r + 1, 1), :], rows[pl.ds(r - 1, 1), :]

            def flag(x):
                return jnp.where(kk < x, 1.0, 0.0)

            wet = flag(c)
            vu = jnp.where(kk >= 1.0, vertical_mixing * wet, 0.0)
            vd = vertical_mixing * flag(c - 1.0)
            drag = jnp.where(kk == c - 1.0, 1.0 - drag_rate, 1.0)
            for q, x in enumerate(
                (
                    flag(jnp.minimum(c, e)), flag(jnp.minimum(c, w)), flag(jnp.minimum(c, n)), flag(jnp.minimum(c, s)),
                    vu, vd, wet - vu - vd, wet * drag,
                )
            ):
                store[q, pl.ds(at, K), :] = x[:K]
        row = j * R + r - G
        row = jnp.where(row >= total_rows, 2 * total_rows - 1 - row, row)
        f = rotation * (2.0 * (row.astype(jnp.float32) + 0.5) / total_rows - 1.0)
        cor[pl.ds(at, K), :] = jnp.full((K, 128), 1.0, jnp.float32) * f

    def pressure(s, start, count, stride):
        for st, out in ((m_st, pm), (q_st, pq)):
            total = None
            for k in range(K):
                sl = pl.ds(start + k, count, stride=stride)
                x = density(st[s, 0, sl, :], st[s, 1, sl, :])
                total = x if total is None else total + x
                out[s, sl, :] = total

    def update(s, b, size, with_q, keep):
        first, last = firstb[:size], lastb[:size]
        sl = pl.ds(b, size)
        mc = [m_st[s, f, sl, :] for f in range(4)] + [pm[s, sl, :]]
        qc = [q_st[s, f, sl, :] for f in range(4)] + [pq[s, sl, :]]
        m_e, m_w, q_e, q_w = [], [], [], []
        for m, q in zip(mc, qc):
            me, mw = pltpu.roll(m, 127, 1), pltpu.roll(m, 1, 1)
            qe, qw = pltpu.roll(q, 127, 1), pltpu.roll(q, 1, 1)
            m_e.append(jnp.where(last, qe, me))
            m_w.append(jnp.where(first, qw, mw))
            if with_q:
                q_e.append(jnp.where(last, me, qe))
                q_w.append(jnp.where(first, mw, qw))
        work = [(m_st, pm, mk, mc, m_e, m_w)]
        if with_q:
            work.append((q_st, pq, qk, qc, q_e, q_w))
        for st, pr, mask, c, e, w in work:
            fe, fw, fn, fs, vu, vd, w0, wd = [mask[q, sl, :] for q in range(N_MASK)]
            a, b_ = courant * c[2], courant * c[3]
            a_neg, b_neg = jnp.minimum(a, 0.0), jnp.minimum(b_, 0.0)
            ce = fe * (mixing - a_neg)
            cw = fw * (mixing + (a - a_neg))
            cn = fn * (mixing - b_neg)
            cs = fs * (mixing + (b_ - b_neg))
            c0 = w0 - ((ce + cw) + (cn + cs))
            north_sl, south_sl = pl.ds(b + K, size), pl.ds(b - K, size)
            new = []
            for f in range(4):
                x = (c0 * c[f] + ce * e[f]) + (cw * w[f] + cn * st[s, f, north_sl, :])
                x = x + (cs * st[s, f, south_sl, :] + vu * st[s, f, pl.ds(b - 1, size), :])
                new.append(x + vd * st[s, f, pl.ds(b + 1, size), :])
            p = c[4]
            px = fe * (e[4] - p) + fw * (p - w[4])
            py = fn * (pr[s, north_sl, :] - p) + fs * (p - pr[s, south_sl, :])
            f0 = cor[sl, :]
            new[2] = wd * (new[2] + f0 * c[3] - px)
            new[3] = wd * (new[3] - f0 * c[2] - py)
            for f in range(4):
                if s < SWEEPS - 1:
                    st[s + 1, f, pl.ds(b, keep), :] = new[f][:keep]
                else:
                    m4[f, pl.ds(b - G * K, keep), :] = new[f][:keep]

    def mask_loop(lo, hi):
        def body(r, carry):
            masks(r)
            return carry

        lax.fori_loop(lo, hi, body, 0)

    sides_of_bottom((G, G + 8))
    mask_loop(G + 1, G + R - 1)
    for s in range(SWEEPS):
        count = R - 2 * s
        pressure(s, (G + s) * K, 8, K)
        pressure(s, (G + R - s - 8) * K, 8, K)
        lo, hi = (G + s + 1) * K, (G + R - s - 1) * K
        steps = -(-(hi - lo) // BLOCK)

        def body(t, carry, s=s, lo=lo, hi=hi):
            b = jnp.minimum(lo + t * BLOCK, hi - BLOCK)
            update(s, b, BLOCK, s < SWEEPS - 1, BLOCK)
            return carry

        lax.fori_loop(0, steps, body, 0)
        if s in (0, 1):
            pass_on(s + 2)

    def unpack_rows(d):
        for f in range(4):
            src = pl.ds(HEAD + (d - 1) * 100 + f * K, K)
            m_st[0, f, pl.ds((G + R - 1 + d) * K, K), :] = recv_n[src, :]

        @pl.when(has_south)
        def _():
            for f in range(4):
                src = pl.ds(HEAD + (d - 1) * 100 + f * K, K)
                m_st[0, f, pl.ds((G - d) * K, K), :] = recv_s[src, :]

    def unpack_corner(src, row_of):
        edge = pltpu.roll(src[pl.ds(24, 8), :], 124, 1)
        for d in range(1, G + 1):
            bq[pl.ds(row_of(d), 1), :] = edge[d - 1 : d]
        for d in range(1, G):
            both = src[pl.ds(8 * (d - 1), 8), :]
            for g in range(16):
                f, kb = g // 4, KB[g % 4]
                q_st[0, f, pl.ds(row_of(d) * K + kb, 8), :] = pltpu.roll(both, (124 - 8 * g) % 128, 1)

    def north_row(d):
        return G + R - 1 + d

    def south_row(d):
        return G - d

    wait_rows(0)
    wait_rows(4)
    for d in range(1, G + 1):
        bm[pl.ds(north_row(d), 1), :] = recv_n[pl.ds(d - 1, 1), :]
    unpack_corner(crecv_n, north_row)

    @pl.when(has_south)
    def _():
        for d in range(1, G + 1):
            bm[pl.ds(south_row(d), 1), :] = recv_s[pl.ds(d - 1, 1), :]
        unpack_corner(crecv_s, south_row)

    sides_of_bottom((0, 16))
    mask_loop(1, G + 1)
    mask_loop(G + R - 1, 2 * G + R - 1)
    for d in range(1, G):
        if d > 1:
            wait_rows(d - 1)
        unpack_rows(d)
    for s in range(SWEEPS):
        for row in (south_row(G - 1 - s), north_row(1 - s)):
            pressure(s, row * K, 3, K)
        for row in (south_row(2 - s), north_row(-s)):
            for b in (row * K, row * K + 35):
                update(s, b, 40, s < SWEEPS - 1, 40)

    wait_rows(G - 1)
    unpack_rows(G)
    for s in range(SWEEPS):
        d = G - s
        pressure(s, south_row(d) * K, 2, (north_row(d) - south_row(d)) * K)
        for row in (south_row(d - 1), north_row(d - 1)):
            update(s, row * K, 32, False, K)

    to_east.wait_send()
    to_west.wait_send()
    for q in range(G):

        @pl.when(passes)
        def _():
            passed(q).wait_send()

    for q in range(G + 1):
        wait_sent(q)


def write_out(m4, t_out, s_out, u_out, v_out):
    for f, out in enumerate((t_out, s_out, u_out, v_out)):
        for k in range(K):
            for h in range(2):
                out[k, pl.ds(8 * h, 8), :] = m4[f, pl.ds(8 * h * K + k, 8, stride=K), :]


def per_device(n_lon, n_lat, t, s, u, v, water_indicator, bottom):
    del water_indicator
    f32 = jnp.float32
    hbm = pl.BlockSpec(memory_space=pl.ANY)
    vmem = pltpu.VMEM
    dma = pltpu.SemaphoreType.DMA
    states = pl.pallas_call(
        functools.partial(kernel, n_lon, n_lat),
        out_shape=pltpu.VMEM((4, R * K, 128), f32),
        in_specs=[hbm] * 5,
        out_specs=pl.BlockSpec(memory_space=pltpu.VMEM),
        scratch_shapes=[
            vmem((4, K, R, 128), f32), vmem((R, 128), jnp.int32),
            vmem((SWEEPS, 4, LIN, 128), f32), vmem((SWEEPS, 4, LIN, 128), f32),
            vmem((SWEEPS, LIN, 128), f32), vmem((SWEEPS, LIN, 128), f32),
            vmem((N_MASK, LIN, 128), f32), vmem((N_MASK, LIN, 128), f32), vmem((LIN, 128), f32),
            vmem((32, 128), f32), vmem((32, 128), f32), vmem((4, 32, 128), f32),
            vmem((PACKED, 128), f32), vmem((PACKED, 128), f32), vmem((PACKED, 128), f32),
            *[vmem((MSG, 128), f32)] * 5,
            vmem((CORNER, 128), f32), vmem((CORNER, 128), f32), vmem((CORNER, 128), f32), vmem((CORNER, 128), f32),
            dma((5,)), dma((2,)), dma((2,)), dma((5,)), dma((5,)), dma((5,)), dma((5,)), dma((G,)), dma((G,)),
        ],
        compiler_params=pltpu.CompilerParams(
            collective_id=1, has_side_effects=True, vmem_limit_bytes=48 * 1024 * 1024
        ),
        name="sweeps",
    )(*(pltpu.with_memory_space_constraint(x, pltpu.HBM) for x in (t, s, u, v, bottom)))
    field = jax.ShapeDtypeStruct((K, R, 128), f32)
    return tuple(
        pl.pallas_call(
            write_out,
            out_shape=[field] * 4,
            compiler_params=pltpu.CompilerParams(vmem_limit_bytes=16 * 1024 * 1024),
            name="write_out",
        )(states)
    )


def solution(mesh):
    field = P(None, LAT, LON)
    return jax.shard_map(
        functools.partial(per_device, mesh.shape[LON], mesh.shape[LAT]),
        mesh=mesh,
        in_specs=(field,) * 5 + (P(LAT, LON),),
        out_specs=(field,) * 4,
        check_vma=False,
    )
```

```python
import functools

import jax
import jax.numpy as jnp
from jax import lax
from jax.experimental import pallas as pl
from jax.experimental.pallas import tpu as pltpu
from jax.sharding import PartitionSpec as P

SWEEPS = 4

courant = 0.3
mixing = 0.08
vertical_mixing = 0.1
buoyancy = 0.05
rotation = 0.2
drag_rate = 0.3
thermal = 0.25
haline = 0.2
cabbeling = 0.03

K = 25
R = 16
G = 4
LIN = (R + 2 * G) * K + 16
BLOCK = 56
HEAD = 8
CHUNKS = ((0, 112), (112, 96), (208, 104), (312, 96))
MSG = 408
PACKED = 104
CORNER = 32
KB = (0, 8, 16, 17)
N_MASK = 8

LON, LAT = "lon", "lat"


def lane(shape):
    return lax.broadcasted_iota(jnp.int32, shape, 1)


def density(t, s):
    h = 0.5 * buoyancy
    return t * (-thermal * h - (cabbeling * h) * t) + (haline * h) * s


def kernel(
    n_lon, n_lat, t_hbm, s_hbm, u_hbm, v_hbm, b_hbm, m4,
    xin, bin_, m_st, q_st, pm, pq, mk, qk, cor, bm, bq, b_side,
    pack, pack_w, pack_e, send_n, send_s, recv_n, recv_s, csend_n, csend_s, crecv_n, crecv_s,
    in_sem, lon_ss, lon_rs, n_ss, n_rs, s_ss, s_rs,
):
    i = lax.axis_index(LON)
    j = lax.axis_index(LAT)
    top = j == n_lat - 1
    east = lax.rem(i + 1, n_lon)
    west = lax.rem(i + n_lon - 1, n_lon)
    has_south = j > 0
    north = {LON: jnp.where(top, n_lon - 1 - i, i), LAT: jnp.where(top, j, j + 1)}
    south = {LON: i, LAT: jnp.maximum(j - 1, 0)}
    mesh_id = pl.DeviceIdType.MESH

    barrier = pltpu.get_barrier_semaphore()
    pl.semaphore_signal(barrier, inc=1, device_id={LON: east, LAT: j}, device_id_type=mesh_id)
    pl.semaphore_signal(barrier, inc=1, device_id={LON: west, LAT: j}, device_id_type=mesh_id)
    pl.semaphore_signal(barrier, inc=1, device_id=north, device_id_type=mesh_id)

    @pl.when(has_south)
    def _():
        pl.semaphore_signal(barrier, inc=1, device_id=south, device_id_type=mesh_id)

    loads = [
        pltpu.make_async_copy(ref, xin.at[f], in_sem.at[f])
        for f, ref in enumerate((t_hbm, s_hbm, u_hbm, v_hbm))
    ]
    loads.append(pltpu.make_async_copy(b_hbm, bin_, in_sem.at[4]))
    for c in loads:
        c.start()
    for c in loads:
        c.wait()

    lanes8 = lane((8, 128))
    group8 = lanes8 // 8

    bm[pl.ds(G, R), :] = bin_[...].astype(jnp.float32)
    tiles = [(f, k, h) for f in range(4) for k in range(K) for h in range(2)]
    tiles += [(4, 0, 0), (4, 0, 1)]
    acc = None
    for n, (f, k, h) in enumerate(tiles):
        if f < 4:
            v = xin[f, k, pl.ds(8 * h, 8), :]
            m_st[0, f, pl.ds((G + 8 * h) * K + k, 8, stride=K), :] = v
        else:
            v = bm[pl.ds(G + 8 * h, 8), :]
        g = n % 16
        rolled = pltpu.roll(v, 4 + 8 * g, 1)
        acc = rolled if g == 0 else jnp.where(group8 == g, rolled, acc)
        if g == 15 or n == len(tiles) - 1:
            pack[pl.ds(8 * (n // 16), 8), :] = acc

    sign = jnp.where(top, -1.0, 1.0).astype(jnp.float32)
    lanes32 = lane((32, 128))
    turn32 = jnp.where(top, 127 - lanes32, lanes32)
    turn8 = jnp.where(top, 127 - lanes8, lanes8)
    sub8 = lax.broadcasted_iota(jnp.int32, (8, 128), 0)

    def turned(v, idx):
        return jnp.take_along_axis(v, idx, axis=1, mode="promise_in_bounds")

    edge = jnp.zeros((8, 128), jnp.float32)
    for d in range(1, G + 1):
        edge = jnp.where(sub8 == d - 1, bm[pl.ds(G + R - d, 1), :], edge)
    send_n[pl.ds(0, 8), :] = turned(edge, turn8)
    send_s[pl.ds(0, 8), :] = bm[pl.ds(G, 8), :]
    for d in range(1, G + 1):
        for f in range(4):
            at = HEAD + (d - 1) * 100 + f * K
            v = turned(m_st[0, f, pl.ds((G + R - d) * K, 32), :], turn32)
            if f >= 2:
                v = v * sign
            send_n[pl.ds(at, K), :] = v[:K]
            send_s[pl.ds(at, K), :] = m_st[0, f, pl.ds((G + d - 1) * K, K), :]

    pl.semaphore_wait(barrier, jnp.where(has_south, 4, 3))

    def remote(src, dst, ss, rs, to):
        return pltpu.make_async_remote_copy(
            src_ref=src, dst_ref=dst, send_sem=ss, recv_sem=rs, device_id=to, device_id_type=mesh_id
        )

    to_east = remote(pack, pack_w, lon_ss.at[0], lon_rs.at[0], {LON: east, LAT: j})
    to_west = remote(pack, pack_e, lon_ss.at[1], lon_rs.at[1], {LON: west, LAT: j})
    to_east.start()
    to_west.start()

    def row_pieces(q):
        if q < G:
            sl = pl.ds(*CHUNKS[q])
            return send_n.at[sl], send_s.at[sl], recv_n.at[sl], recv_s.at[sl]
        return csend_n, csend_s, crecv_n, crecv_s

    def start_rows(q):
        sn, ss, rn, rs = row_pieces(q)

        @pl.when(jnp.logical_not(top))
        def _():
            remote(sn, rs, n_ss.at[q], s_rs.at[q], north).start()

        @pl.when(top)
        def _():
            remote(sn, rn, n_ss.at[q], n_rs.at[q], north).start()

        @pl.when(has_south)
        def _():
            remote(ss, rn, s_ss.at[q], n_rs.at[q], south).start()

    def wait_rows(q):
        sn, ss, rn, rs = row_pieces(q)
        remote(ss, rn, s_ss.at[q], n_rs.at[q], north).wait_recv()

        @pl.when(has_south)
        def _():
            remote(sn, rs, n_ss.at[q], s_rs.at[q], south).wait_recv()

    def wait_sent(q):
        sn, ss, rn, rs = row_pieces(q)
        remote(sn, rs, n_ss.at[q], s_rs.at[q], north).wait_send()

        @pl.when(has_south)
        def _():
            remote(ss, rn, s_ss.at[q], n_rs.at[q], south).wait_send()

    start_rows(0)
    start_rows(1)

    @pl.when(jnp.logical_not(has_south))
    def _():
        zero = jnp.zeros((G * K, 128), jnp.float32)
        bm[pl.ds(0, G), :] = zero[:G]
        bq[pl.ds(0, G), :] = zero[:G]
        for f in range(4):
            m_st[0, f, pl.ds(0, G * K), :] = zero
            q_st[0, f, pl.ds(0, G * K), :] = zero

    to_east.wait_recv()
    to_west.wait_recv()
    west_half = lanes8 % 8 < 4
    for q in range(PACKED // 8):
        both = jnp.where(west_half, pack_w[pl.ds(8 * q, 8), :], pack_e[pl.ds(8 * q, 8), :])
        for g in range(16):
            n = 16 * q + g
            if n >= len(tiles):
                break
            f, k, h = tiles[n]
            v = pltpu.roll(both, (124 - 8 * g) % 128, 1)
            if f < 4:
                q_st[0, f, pl.ds((G + 8 * h) * K + k, 8, stride=K), :] = v
            else:
                bq[pl.ds(G + 8 * h, 8), :] = v

    flip8 = jnp.where(top, lanes8 + 7 - 2 * (lanes8 % 8), lanes8)
    sign8 = jnp.where(lanes8 >= 64, sign, 1.0)
    for d in range(1, G):
        acc_n = acc_s = None
        for g in range(16):
            f, kb = g // 4, KB[g % 4]
            vn = pltpu.roll(q_st[0, f, pl.ds((G + R - d) * K + kb, 8), :], 4 + 8 * g, 1)
            vs = pltpu.roll(q_st[0, f, pl.ds((G + d - 1) * K + kb, 8), :], 4 + 8 * g, 1)
            acc_n = vn if g == 0 else jnp.where(group8 == g, vn, acc_n)
            acc_s = vs if g == 0 else jnp.where(group8 == g, vs, acc_s)
        csend_n[pl.ds(8 * (d - 1), 8), :] = turned(acc_n, flip8) * sign8
        csend_s[pl.ds(8 * (d - 1), 8), :] = acc_s
    edge = jnp.zeros((8, 128), jnp.float32)
    for d in range(1, G + 1):
        edge = jnp.where(sub8 == d - 1, bq[pl.ds(G + R - d, 1), :], edge)
    csend_n[pl.ds(24, 8), :] = turned(pltpu.roll(edge, 4, 1), flip8)
    csend_s[pl.ds(24, 8), :] = pltpu.roll(bq[pl.ds(G, 8), :], 4, 1)
    start_rows(4)
    start_rows(2)
    start_rows(3)

    kk = lax.broadcasted_iota(jnp.int32, (32, 128), 0).astype(jnp.float32)
    firstb = lane((BLOCK, 128)) == 0
    lastb = lane((BLOCK, 128)) == 127
    total_rows = n_lat * R

    def sides_of_bottom(rows):
        for r in rows:
            sl = pl.ds(r, 8)
            m, q = bm[sl, :], bq[sl, :]
            first, last = lanes8 == 0, lanes8 == 127
            b_side[0, sl, :] = pltpu.roll(jnp.where(first, q, m), 127, 1)
            b_side[1, sl, :] = pltpu.roll(jnp.where(last, q, m), 1, 1)
            b_side[2, sl, :] = pltpu.roll(jnp.where(first, m, q), 127, 1)
            b_side[3, sl, :] = pltpu.roll(jnp.where(last, m, q), 1, 1)

    def masks(r):
        at = r * K
        one = pl.ds(r, 1)
        sides = (
            (mk, bm[one, :], b_side[0, one, :], b_side[1, one, :], bm),
            (qk, bq[one, :], b_side[2, one, :], b_side[3, one, :], bq),
        )
        for store, c, e, w, rows in sides:
            n, s = rows[pl.ds(r + 1, 1), :], rows[pl.ds(r - 1, 1), :]

            def flag(x):
                return jnp.where(kk < x, 1.0, 0.0)

            wet = flag(c)
            vu = jnp.where(kk >= 1.0, vertical_mixing * wet, 0.0)
            vd = vertical_mixing * flag(c - 1.0)
            drag = jnp.where(kk == c - 1.0, 1.0 - drag_rate, 1.0)
            for q, x in enumerate(
                (
                    flag(jnp.minimum(c, e)), flag(jnp.minimum(c, w)), flag(jnp.minimum(c, n)), flag(jnp.minimum(c, s)),
                    vu, vd, wet - vu - vd, wet * drag,
                )
            ):
                store[q, pl.ds(at, K), :] = x[:K]
        row = j * R + r - G
        row = jnp.where(row >= total_rows, 2 * total_rows - 1 - row, row)
        f = rotation * (2.0 * (row.astype(jnp.float32) + 0.5) / total_rows - 1.0)
        cor[pl.ds(at, K), :] = jnp.full((K, 128), 1.0, jnp.float32) * f

    def pressure(s, start, count, stride):
        for st, out in ((m_st, pm), (q_st, pq)):
            total = None
            for k in range(K):
                sl = pl.ds(start + k, count, stride=stride)
                x = density(st[s, 0, sl, :], st[s, 1, sl, :])
                total = x if total is None else total + x
                out[s, sl, :] = total

    def update(s, b, size, with_q, keep):
        first, last = firstb[:size], lastb[:size]
        sl = pl.ds(b, size)
        mc = [m_st[s, f, sl, :] for f in range(4)] + [pm[s, sl, :]]
        qc = [q_st[s, f, sl, :] for f in range(4)] + [pq[s, sl, :]]
        m_e, m_w, q_e, q_w = [], [], [], []
        for m, q in zip(mc, qc):
            me, mw = pltpu.roll(m, 127, 1), pltpu.roll(m, 1, 1)
            qe, qw = pltpu.roll(q, 127, 1), pltpu.roll(q, 1, 1)
            m_e.append(jnp.where(last, qe, me))
            m_w.append(jnp.where(first, qw, mw))
            if with_q:
                q_e.append(jnp.where(last, me, qe))
                q_w.append(jnp.where(first, mw, qw))
        work = [(m_st, pm, mk, mc, m_e, m_w)]
        if with_q:
            work.append((q_st, pq, qk, qc, q_e, q_w))
        for st, pr, mask, c, e, w in work:
            fe, fw, fn, fs, vu, vd, w0, wd = [mask[q, sl, :] for q in range(N_MASK)]
            a, b_ = courant * c[2], courant * c[3]
            a_neg, b_neg = jnp.minimum(a, 0.0), jnp.minimum(b_, 0.0)
            ce = fe * (mixing - a_neg)
            cw = fw * (mixing + (a - a_neg))
            cn = fn * (mixing - b_neg)
            cs = fs * (mixing + (b_ - b_neg))
            c0 = w0 - ((ce + cw) + (cn + cs))
            north_sl, south_sl = pl.ds(b + K, size), pl.ds(b - K, size)
            new = []
            for f in range(4):
                x = (c0 * c[f] + ce * e[f]) + (cw * w[f] + cn * st[s, f, north_sl, :])
                x = x + (cs * st[s, f, south_sl, :] + vu * st[s, f, pl.ds(b - 1, size), :])
                new.append(x + vd * st[s, f, pl.ds(b + 1, size), :])
            p = c[4]
            px = fe * (e[4] - p) + fw * (p - w[4])
            py = fn * (pr[s, north_sl, :] - p) + fs * (p - pr[s, south_sl, :])
            f0 = cor[sl, :]
            new[2] = wd * (new[2] + f0 * c[3] - px)
            new[3] = wd * (new[3] - f0 * c[2] - py)
            for f in range(4):
                if s < SWEEPS - 1:
                    st[s + 1, f, pl.ds(b, keep), :] = new[f][:keep]
                else:
                    m4[f, pl.ds(b - G * K, keep), :] = new[f][:keep]

    def mask_loop(lo, hi):
        def body(r, carry):
            masks(r)
            return carry

        lax.fori_loop(lo, hi, body, 0)

    sides_of_bottom((G, G + 8))
    mask_loop(G + 1, G + R - 1)
    for s in range(SWEEPS):
        count = R - 2 * s
        pressure(s, (G + s) * K, 8, K)
        pressure(s, (G + R - s - 8) * K, 8, K)
        lo, hi = (G + s + 1) * K, (G + R - s - 1) * K
        steps = -(-(hi - lo) // BLOCK)

        def body(t, carry, s=s, lo=lo, hi=hi):
            b = jnp.minimum(lo + t * BLOCK, hi - BLOCK)
            update(s, b, BLOCK, s < SWEEPS - 1, BLOCK)
            return carry

        lax.fori_loop(0, steps, body, 0)

    def unpack_rows(d):
        for f in range(4):
            src = pl.ds(HEAD + (d - 1) * 100 + f * K, K)
            m_st[0, f, pl.ds((G + R - 1 + d) * K, K), :] = recv_n[src, :]

        @pl.when(has_south)
        def _():
            for f in range(4):
                src = pl.ds(HEAD + (d - 1) * 100 + f * K, K)
                m_st[0, f, pl.ds((G - d) * K, K), :] = recv_s[src, :]

    def unpack_corner(src, row_of):
        edge = pltpu.roll(src[pl.ds(24, 8), :], 124, 1)
        for d in range(1, G + 1):
            bq[pl.ds(row_of(d), 1), :] = edge[d - 1 : d]
        for d in range(1, G):
            both = src[pl.ds(8 * (d - 1), 8), :]
            for g in range(16):
                f, kb = g // 4, KB[g % 4]
                q_st[0, f, pl.ds(row_of(d) * K + kb, 8), :] = pltpu.roll(both, (124 - 8 * g) % 128, 1)

    def north_row(d):
        return G + R - 1 + d

    def south_row(d):
        return G - d

    for e in range(1, G + 1):
        wait_rows(e - 1)
        unpack_rows(e)
        if e == 1:
            wait_rows(4)
            for d in range(1, G + 1):
                bm[pl.ds(north_row(d), 1), :] = recv_n[pl.ds(d - 1, 1), :]
            unpack_corner(crecv_n, north_row)

            @pl.when(has_south)
            def _():
                for d in range(1, G + 1):
                    bm[pl.ds(south_row(d), 1), :] = recv_s[pl.ds(d - 1, 1), :]
                unpack_corner(crecv_s, south_row)

            sides_of_bottom((0, 16))
            mask_loop(1, G + 1)
            mask_loop(G + R - 1, 2 * G + R - 1)
        for s in range(SWEEPS):
            d = e - s
            pressure(s, south_row(d) * K, 2, (north_row(d) - south_row(d)) * K)
            for row in (south_row(d - 1), north_row(d - 1)):
                update(s, row * K, 32, s < SWEEPS - 1 and e < G, K)

    to_east.wait_send()
    to_west.wait_send()
    for q in range(G + 1):
        wait_sent(q)


def write_out(m4, t_out, s_out, u_out, v_out):
    for f, out in enumerate((t_out, s_out, u_out, v_out)):
        for k in range(K):
            for h in range(2):
                out[k, pl.ds(8 * h, 8), :] = m4[f, pl.ds(8 * h * K + k, 8, stride=K), :]


def per_device(n_lon, n_lat, t, s, u, v, water_indicator, bottom):
    del water_indicator
    f32 = jnp.float32
    hbm = pl.BlockSpec(memory_space=pl.ANY)
    vmem = pltpu.VMEM
    dma = pltpu.SemaphoreType.DMA
    states = pl.pallas_call(
        functools.partial(kernel, n_lon, n_lat),
        out_shape=pltpu.VMEM((4, R * K, 128), f32),
        in_specs=[hbm] * 5,
        out_specs=pl.BlockSpec(memory_space=pltpu.VMEM),
        scratch_shapes=[
            vmem((4, K, R, 128), f32), vmem((R, 128), jnp.int32),
            vmem((SWEEPS, 4, LIN, 128), f32), vmem((SWEEPS, 4, LIN, 128), f32),
            vmem((SWEEPS, LIN, 128), f32), vmem((SWEEPS, LIN, 128), f32),
            vmem((N_MASK, LIN, 128), f32), vmem((N_MASK, LIN, 128), f32), vmem((LIN, 128), f32),
            vmem((32, 128), f32), vmem((32, 128), f32), vmem((4, 32, 128), f32),
            vmem((PACKED, 128), f32), vmem((PACKED, 128), f32), vmem((PACKED, 128), f32),
            vmem((MSG, 128), f32), vmem((MSG, 128), f32), vmem((MSG, 128), f32), vmem((MSG, 128), f32),
            vmem((CORNER, 128), f32), vmem((CORNER, 128), f32), vmem((CORNER, 128), f32), vmem((CORNER, 128), f32),
            dma((5,)), dma((2,)), dma((2,)), dma((5,)), dma((5,)), dma((5,)), dma((5,)),
        ],
        compiler_params=pltpu.CompilerParams(
            collective_id=1, has_side_effects=True, vmem_limit_bytes=48 * 1024 * 1024
        ),
        name="sweeps",
    )(*(pltpu.with_memory_space_constraint(x, pltpu.HBM) for x in (t, s, u, v, bottom)))
    field = jax.ShapeDtypeStruct((K, R, 128), f32)
    return tuple(
        pl.pallas_call(
            write_out,
            out_shape=[field] * 4,
            compiler_params=pltpu.CompilerParams(vmem_limit_bytes=16 * 1024 * 1024),
            name="write_out",
        )(states)
    )


def solution(mesh):
    field = P(None, LAT, LON)
    return jax.shard_map(
        functools.partial(per_device, mesh.shape[LON], mesh.shape[LAT]),
        mesh=mesh,
        in_specs=(field,) * 5 + (P(LAT, LON),),
        out_specs=(field,) * 4,
        check_vma=False,
    )
```
